32 devices in a mesh: parts: 2 (over y), dp: 8 (over z, x), tensor: 2 (over core).
Axes of the slice: x: 2, y: 2, z: 4, core: 2. Of those that a mesh axis runs over, the one named last changes fastest.
Arguments:
- activations: bfloat16 [2, 8192, 25600], P(None, ('parts', 'dp'), 'tensor'), parts along dimension 1, may hold values from -6 to 6
- out_grads: bfloat16 [2, 8192, 5120], P(None, ('parts', 'dp'), 'tensor'), parts along dimension 1, may hold values from -6 to 6
- proj_in: bfloat16 [25600, 64], P('tensor'), may hold values from -0.0390625 to 0.0390625
- proj_out: bfloat16 [5120, 64], P('tensor'), may hold values from -0.078125 to 0.078125
- token_ids: int32 [32, 256], P(('parts', 'dp')), parts along dimension 0, may hold values from 0 to 151643, as said below
- queries: bfloat16 [2, 2048, 4096], P(None, 'tensor', 'dp'), may hold values from -6 to 6
- query_docs: int32 [4096, 8], P(('parts', 'tensor')), parts along dimension 0, may hold values from 0 to 15, all different within a row
Outputs:
- scores: float32 [32, 2048], P(('parts', 'dp'), 'tensor'), parts along dimension 0
- listed: float32 [4096], P(('parts', 'tensor')), parts along dimension 0
The draws below stay inside these ranges and needn't reach their ends.
There are 2 independent parts, one for each index of `parts`. The reference program is written for one: setup_inputs(seed, part) draws one part's arguments, and reference() takes and returns one part's arrays. A program takes and returns all parts, laid end to end along the dimension named above; an argument that names none is the same for every part. Nothing has to cross between parts.
Inputs may be any that keep to these rules, and one draw needn't show every extreme that they name: `token_ids`: each document is a run of real token ids below 151643 followed by padding id 151643 up to its end; it has at least 64 real tokens, and some document is padded. `query_docs`: each query lists 8 different documents.
All inputs are finite; a program needn't handle non-finite values.
Results may differ from the reference program's by a relative error of at most 0.0029.
Values may be sent and summed in bfloat16 or wider, within the bound.
No kernel may reach another device: no remote copies, remote signals or barrier semaphores. Data moves between devices by JAX's collectives and lax.ppermute only.
A program may use at most 128 MiB of HBM per device.

```python
import jax
import jax.numpy as jnp
from jax import lax

D = 5120
FF = 25600
R = 64
C = 2
DOC_LEN = 256
Q = 2048
K = 8
DOCS = 16
TOKENS = 4096


def draw_token_ids(key, part):
    key = jax.random.fold_in(key, 7)
    len_key, word_key = jax.random.split(key)
    lengths = jax.random.randint(len_key, (DOCS,), DOC_LEN // 4, DOC_LEN + 1)
    lengths = lengths.at[0].set(DOC_LEN // 2)
    words = jax.random.randint(word_key, (DOCS, DOC_LEN), 0, 151643)
    positions = jnp.arange(DOC_LEN)[None, :]
    return jnp.where(positions < lengths[:, None], words, 151643).astype(jnp.int32)


def steps_of(rng, shape, cuts, least, high):
    loudness = 1.0
    for axis_at, shards_of in cuts:
        draws = jax.random.uniform(jax.random.fold_in(jax.random.fold_in(rng, 6), axis_at), (shards_of,), jnp.float32, least / len(cuts), high / len(cuts))
        loudness = loudness * jnp.repeat(jnp.exp(draws), shape[axis_at] // shards_of).reshape((-1,) + (1,) * (len(shape) - 1 - axis_at))
    return loudness


def choose_distinct(stream_key, rows, amount, top, lift):
    ranking = jax.random.permutation(jax.random.fold_in(stream_key, 1), amount)
    favour = ranking
    for power in range(3):
        favour = favour * favour // amount
    favour = favour * lift // amount
    tickets = jax.random.randint(jax.random.fold_in(stream_key, 2), (rows, amount), 0, 4096) + favour
    fixed_rows = jax.random.permutation(jax.random.fold_in(stream_key, 3), rows)[jnp.arange(amount) % rows]
    tickets = jnp.where(jnp.arange(rows)[:, None] == fixed_rows[None, :], 1 << 14, tickets)
    merit = tickets * amount + jnp.arange(amount)
    return lax.top_k(merit.astype(jnp.int32), top)[1].astype(jnp.int32)


def noise(stream_key, dims, width, limit, pieces=(), dtype=jnp.bfloat16):
    drawn = width * jax.random.normal(stream_key, dims, jnp.float32)
    if pieces:
        drawn = drawn * steps_of(stream_key, dims, pieces, -0.22, 0.18)
    return jnp.clip(drawn, -limit, limit).astype(dtype)


def setup_inputs(seed: int = 0, part: int = 0) -> dict:
    key_list = jax.random.split(jax.random.key(seed), 8)
    own_keys = jax.random.split(jax.random.fold_in(key_list[7], part), 8)
    activations = noise(own_keys[0], (C, TOKENS, FF), 1.0, 6.0, ((1, 8), (2, 2)))
    out_grads = noise(own_keys[1], (C, TOKENS, D), 1.0, 6.0, ((1, 8), (2, 2)))
    proj_in = noise(key_list[2], (FF, R), FF ** -0.5, 0.0390625, ((0, 2),))
    proj_out = noise(key_list[3], (D, R), D ** -0.5, 0.078125, ((0, 2),))
    token_ids = draw_token_ids(jax.random.fold_in(jax.random.fold_in(key_list[7], part), 71), part)
    queries = noise(key_list[5], (C, Q, R * R), 1.0, 6.0, ((1, 2), (2, 8)))
    query_docs = choose_distinct(own_keys[6], Q, DOCS, K, 0)
    return {"activations": activations, "out_grads": out_grads, "proj_in": proj_in, "proj_out": proj_out, "token_ids": token_ids, "queries": queries, "query_docs": query_docs}


pad_token = 151643


def reference(activations, out_grads, proj_in, proj_out, token_ids, queries, query_docs):
    in_proj = jnp.stack([jnp.dot(activations[c], proj_in, preferred_element_type=jnp.float32) for c in range(C)])
    out_proj = jnp.stack([jnp.dot(out_grads[c], proj_out, preferred_element_type=jnp.float32) for c in range(C)])
    keep_mask = (token_ids != pad_token).astype(jnp.float32).reshape(1, DOCS, DOC_LEN, 1)
    in_proj = in_proj.reshape(C, DOCS, DOC_LEN, R)
    out_proj = out_proj.reshape(C, DOCS, DOC_LEN, R) * keep_mask
    doc_grads = jnp.einsum("cntr,cnts->cnrs", out_proj, in_proj, precision=lax.Precision.HIGHEST)
    doc_grads = (doc_grads * (DOC_LEN ** -0.5)).reshape(C, DOCS, R * R).astype(jnp.bfloat16)
    scores = jnp.einsum("cnf,cqf->nq", doc_grads.astype(jnp.float32), queries.astype(jnp.float32), precision=lax.Precision.HIGHEST) / R
    picked = jnp.take_along_axis(scores.T, query_docs, axis=1)
    listed = jnp.sum(picked, axis=1) / K
    return scores, listed
```

```python
import jax
import jax.numpy as jnp
from jax import lax
from jax.sharding import PartitionSpec as P

PAD = 151643


def sum_over_tensor(part, size):
    if size == 2:
        return part + lax.ppermute(part, "tensor", [(0, 1), (1, 0)])
    return lax.psum(part, "tensor")


def body(dp, tensor, activations, out_grads, proj_in, proj_out, token_ids, queries, query_docs):
    checkpoints = activations.shape[0]
    rank = proj_in.shape[1]
    docs, doc_len = token_ids.shape
    rows = rank // dp
    own_queries = queries.shape[1]

    out_part = jnp.einsum("ctd,dr->ctr", out_grads, proj_out, preferred_element_type=jnp.float32)
    out_proj = sum_over_tensor(out_part, tensor)
    in_part = jnp.einsum("ctf,fr->ctr", activations, proj_in, preferred_element_type=jnp.float32)
    keep = (token_ids != PAD).astype(jnp.float32).reshape(1, docs, doc_len, 1)
    out_proj = out_proj.reshape(checkpoints, docs, doc_len, rank) * keep
    in_part = in_part.reshape(checkpoints, docs, doc_len, rank)
    term = jnp.einsum("cntr,cnts->crns", out_proj, in_part, precision=lax.Precision.HIGHEST)
    term = term.reshape(checkpoints, dp, 1, rows, docs * rank).transpose(1, 2, 0, 3, 4)
    term = jnp.broadcast_to(term, (dp, tensor, checkpoints, rows, docs * rank))
    term = term.reshape(dp * tensor, checkpoints, rows, docs * rank)
    terms = lax.all_to_all(term, ("dp", "tensor"), 0, 0, tiled=True)
    grads = terms.reshape(dp, tensor, checkpoints, rows, docs, rank).sum(1) * doc_len ** (-0.5)
    grads = grads.astype(jnp.bfloat16).transpose(1, 0, 3, 2, 4).reshape(checkpoints, dp * docs, rows * rank)

    part = jnp.einsum("cnf,cqf->nq", grads, queries, preferred_element_type=jnp.float32)
    every_doc = jnp.arange(dp * docs, dtype=jnp.int32)
    listing = (query_docs.T[None] == every_doc[:, None, None]).sum(1).astype(jnp.float32)
    listed_part = (listing * part).sum(0)
    sent = jnp.concatenate(
        [
            part.reshape(dp, docs, own_queries),
            jnp.broadcast_to(listed_part, (dp, 1, own_queries)),
        ],
        axis=1,
    )
    total = lax.all_to_all(sent, "dp", 0, 0, tiled=True).sum(0) / rank
    return total[:docs], total[docs] / query_docs.shape[1]


def solution(mesh):
    dp, tensor = mesh.shape["dp"], mesh.shape["tensor"]
    in_specs = (
        P(None, ("parts", "dp"), "tensor"),
        P(None, ("parts", "dp"), "tensor"),
        P("tensor", None),
        P("tensor", None),
        P(("parts", "dp"), None),
        P(None, "tensor", "dp"),
        P(("parts", "tensor"), None),
    )
    out_specs = (P(("parts", "dp"), "tensor"), P(("parts", "tensor")))
    return jax.shard_map(
        lambda *arrays: body(dp, tensor, *arrays),
        mesh=mesh,
        in_specs=in_specs,
        out_specs=out_specs,
        check_vma=False,
    )
```

```python
import functools

import jax
import jax.numpy as jnp
from jax import lax
from jax.experimental import pallas as pl
from jax.experimental.pallas import tpu as pltpu
from jax.sharding import PartitionSpec as P

PAD = 151643
BLOCK = 128
VMEM = pl.BlockSpec(memory_space=pltpu.VMEM)
HBM = pl.BlockSpec(memory_space=pltpu.HBM)
LAST = (((1,), (1,)), ((), ()))


def project_kernel(
    doc_len, acts_ref, outs_ref, in_ref, out_ref, mine_ref, theirs_ref, acts, outs, infac, outfac, act_sems, out_sems, fac_sems
):
    checkpoints, tokens, _ = acts.shape
    rank = infac.shape[0]
    half = checkpoints * rank
    steps = tokens // BLOCK
    keeps = lax.axis_index("tensor")

    def rows_of(i):
        return pl.ds(pl.multiple_of(i * BLOCK, BLOCK), BLOCK)

    def out_copy(i, c):
        return pltpu.make_async_copy(outs_ref.at[c, rows_of(i)], outs.at[c, rows_of(i)], out_sems.at[i, c])

    def act_copy(i, c):
        return pltpu.make_async_copy(acts_ref.at[c, rows_of(i)], acts.at[c, rows_of(i)], act_sems.at[i, c])

    out_fac_copy = pltpu.make_async_copy(out_ref, outfac, fac_sems.at[0])
    in_fac_copy = pltpu.make_async_copy(in_ref, infac, fac_sems.at[1])

    def start_outs(i, carry):
        for c in range(checkpoints):
            out_copy(i, c).start()
        return carry

    def start_acts(i, carry):
        for c in range(checkpoints):
            act_copy(i, c).start()
        return carry

    out_fac_copy.start()
    lax.fori_loop(0, steps, start_outs, 0)
    in_fac_copy.start()
    lax.fori_loop(0, steps, start_acts, 0)

    def project(i, copy, wide, factor, side):
        for c in range(checkpoints):
            copy(i, c).wait()
        found = [
            lax.dot_general(wide[c, rows_of(i)], factor[...], LAST, preferred_element_type=jnp.float32)
            for c in range(checkpoints)
        ]
        both = jnp.concatenate(found, axis=1)
        doc = i // (doc_len // BLOCK)
        at = pl.ds(pl.multiple_of(i * BLOCK - doc * doc_len, BLOCK), BLOCK)

        @pl.when(doc == keeps)
        def _():
            mine_ref[at, side * half : (side + 1) * half] = both

        @pl.when(doc != keeps)
        def _():
            theirs_ref[at, side * half : (side + 1) * half] = both

    def out_step(i, carry):
        project(i, out_copy, outs, outfac, 0)
        return carry

    def act_step(i, carry):
        project(i, act_copy, acts, infac, 1)
        return carry

    out_fac_copy.wait()
    lax.fori_loop(0, steps, out_step, 0)
    in_fac_copy.wait()
    lax.fori_loop(0, steps, act_step, 0)


def grad_kernel(dp, tensor, checkpoints, ids_ref, mine_ref, other_ref, sent_ref):
    doc_len = mine_ref.shape[0]
    half = mine_ref.shape[1] // 2
    rank = half // checkpoints
    rows = rank // dp
    ids = ids_ref[pl.ds(lax.axis_index("tensor"), 1), :]
    keep = jnp.where(ids != PAD, doc_len**-0.5, 0.0)
    both = mine_ref[...] + other_ref[...]
    kept = both[:, :half].T * keep
    sums = jnp.dot(
        kept, both[:, half:], precision=lax.Precision.HIGHEST, preferred_element_type=jnp.float32
    )
    grads = jnp.concatenate(
        [sums[c * rank : (c + 1) * rank, c * rank : (c + 1) * rank] for c in range(checkpoints)], axis=1
    )
    for j in range(dp):
        for k in range(tensor):
            sent_ref[j * tensor + k] = grads[j * rows : (j + 1) * rows]


def score_kernel(dp, checkpoints, terms_ref, queries_ref, listed_ref, sent_ref):
    all_docs, rows, lanes = terms_ref.shape
    rank = lanes // checkpoints
    docs = all_docs // dp
    parts = [terms_ref[:, r, :].astype(jnp.bfloat16) for r in range(rows)]
    part = None
    for c in range(checkpoints):
        grads = jnp.concatenate([p[:, c * rank : (c + 1) * rank] for p in parts], axis=1)
        term = lax.dot_general(grads, queries_ref[c], LAST, preferred_element_type=jnp.float32)
        part = term if part is None else part + term
    part = part * (1.0 / rank)
    places = listed_ref.shape[0]
    every = lax.broadcasted_iota(jnp.int32, part.shape, 0)
    weight = jnp.zeros(part.shape, jnp.float32)
    for k in range(places):
        weight += jnp.where(listed_ref[k : k + 1, :] == every, 1.0 / places, 0.0)
    own = jnp.sum(weight * part, axis=0, keepdims=True)
    for j in range(dp):
        sent_ref[j, 0:docs, :] = part[j * docs : (j + 1) * docs]
        sent_ref[j, docs : docs + 1, :] = own


def total_kernel(parts_ref, scores_ref, listed_ref):
    docs = scores_ref.shape[0]
    total = parts_ref[0]
    for i in range(1, parts_ref.shape[0]):
        total += parts_ref[i]
    scores_ref[...] = total[:docs]
    listed_ref[...] = total[docs:]


def pair_body(dp, tensor, activations, out_grads, proj_in, proj_out, token_ids, queries, query_docs):
    checkpoints, tokens, _ = activations.shape
    rank = proj_in.shape[1]
    docs, doc_len = token_ids.shape
    rows = rank // dp
    own_queries = queries.shape[1]
    lanes = checkpoints * rank
    steps = tokens // BLOCK
    wide = activations.size + out_grads.size
    f32 = jnp.float32

    side = jax.ShapeDtypeStruct((doc_len, 2 * lanes), f32)
    mine, theirs = pl.pallas_call(
        functools.partial(project_kernel, doc_len),
        in_specs=[HBM] * 4,
        out_specs=[VMEM] * 2,
        out_shape=[pltpu.VMEM(side.shape, f32)] * 2,
        scratch_shapes=[
            pltpu.VMEM(activations.shape, activations.dtype),
            pltpu.VMEM(out_grads.shape, out_grads.dtype),
            pltpu.VMEM(proj_in.shape[::-1], proj_in.dtype),
            pltpu.VMEM(proj_out.shape[::-1], proj_out.dtype),
            pltpu.SemaphoreType.DMA((steps, checkpoints)),
            pltpu.SemaphoreType.DMA((steps, checkpoints)),
            pltpu.SemaphoreType.DMA((2,)),
        ],
        compiler_params=pltpu.CompilerParams(vmem_limit_bytes=40 << 20),
        cost_estimate=pl.CostEstimate(flops=2 * wide * rank, bytes_accessed=2 * wide, transcendentals=0),
        name="project",
    )(*(pltpu.with_memory_space_constraint(x, pltpu.HBM) for x in (activations, out_grads, proj_in.T, proj_out.T)))
    other = lax.ppermute(theirs, "tensor", [(0, 1), (1, 0)])
    sent = pl.pallas_call(
        functools.partial(grad_kernel, dp, tensor, checkpoints),
        in_specs=[VMEM] * 3,
        out_specs=VMEM,
        out_shape=jax.ShapeDtypeStruct((dp * tensor, rows, lanes), f32),
        compiler_params=pltpu.CompilerParams(vmem_limit_bytes=4 << 20),
        name="doc_grads",
    )(token_ids, mine, other)
    terms = lax.all_to_all(sent, ("dp", "tensor"), 0, 0, tiled=True)
    parts = pl.pallas_call(
        functools.partial(score_kernel, dp, checkpoints),
        in_specs=[VMEM] * 3,
        out_specs=VMEM,
        out_shape=jax.ShapeDtypeStruct((dp, docs + 1, own_queries), f32),
        compiler_params=pltpu.CompilerParams(vmem_limit_bytes=8 << 20),
        name="partial_scores",
    )(terms, queries, query_docs.T)
    parts = lax.all_to_all(parts, "dp", 0, 0, tiled=True)
    scores, listed = pl.pallas_call(
        total_kernel,
        in_specs=[VMEM],
        out_specs=[VMEM] * 2,
        out_shape=[jax.ShapeDtypeStruct((docs, own_queries), f32), jax.ShapeDtypeStruct((1, own_queries), f32)],
        compiler_params=pltpu.CompilerParams(vmem_limit_bytes=4 << 20),
        name="totals",
    )(parts)
    return scores, listed.reshape(own_queries)


def sum_over_tensor(part, size):
    if size == 2:
        return part + lax.ppermute(part, "tensor", [(0, 1), (1, 0)])
    return lax.psum(part, "tensor")


def any_body(dp, tensor, activations, out_grads, proj_in, proj_out, token_ids, queries, query_docs):
    checkpoints = activations.shape[0]
    rank = proj_in.shape[1]
    docs, doc_len = token_ids.shape
    rows = rank // dp
    own_queries = queries.shape[1]

    out_part = jnp.einsum("ctd,dr->ctr", out_grads, proj_out, preferred_element_type=jnp.float32)
    out_proj = sum_over_tensor(out_part, tensor)
    in_part = jnp.einsum("ctf,fr->ctr", activations, proj_in, preferred_element_type=jnp.float32)
    keep = (token_ids != PAD).astype(jnp.float32).reshape(1, docs, doc_len, 1)
    out_proj = out_proj.reshape(checkpoints, docs, doc_len, rank) * keep
    in_part = in_part.reshape(checkpoints, docs, doc_len, rank)
    term = jnp.einsum("cntr,cnts->crns", out_proj, in_part, precision=lax.Precision.HIGHEST)
    term = term.reshape(checkpoints, dp, 1, rows, docs * rank).transpose(1, 2, 0, 3, 4)
    term = jnp.broadcast_to(term, (dp, tensor, checkpoints, rows, docs * rank))
    term = term.reshape(dp * tensor, checkpoints, rows, docs * rank)
    terms = lax.all_to_all(term, ("dp", "tensor"), 0, 0, tiled=True)
    grads = terms.reshape(dp, tensor, checkpoints, rows, docs, rank).sum(1) * doc_len ** (-0.5)
    grads = grads.astype(jnp.bfloat16).transpose(1, 0, 3, 2, 4).reshape(checkpoints, dp * docs, rows * rank)

    part = jnp.einsum("cnf,cqf->nq", grads, queries, preferred_element_type=jnp.float32)
    every_doc = jnp.arange(dp * docs, dtype=jnp.int32)
    listing = (query_docs.T[None] == every_doc[:, None, None]).sum(1).astype(jnp.float32)
    listed_part = (listing * part).sum(0)
    sent = jnp.concatenate(
        [
            part.reshape(dp, docs, own_queries),
            jnp.broadcast_to(listed_part, (dp, 1, own_queries)),
        ],
        axis=1,
    )
    total = lax.all_to_all(sent, "dp", 0, 0, tiled=True).sum(0) / rank
    return total[:docs], total[docs] / query_docs.shape[1]


def solution(mesh):
    dp, tensor = mesh.shape["dp"], mesh.shape["tensor"]

    def body(*arrays):
        docs, doc_len = arrays[4].shape
        paired = tensor == 2 and docs == 2 and doc_len % BLOCK == 0
        return (pair_body if paired else any_body)(dp, tensor, *arrays)

    in_specs = (
        P(None, ("parts", "dp"), "tensor"),
        P(None, ("parts", "dp"), "tensor"),
        P("tensor", None),
        P("tensor", None),
        P(("parts", "dp"), None),
        P(None, "tensor", "dp"),
        P(("parts", "tensor"), None),
    )
    out_specs = (P(("parts", "dp"), "tensor"), P(("parts", "tensor")))
    return jax.shard_map(
        body,
        mesh=mesh,
        in_specs=in_specs,
        out_specs=out_specs,
        check_vma=False,
    )
```

```python
import functools

import jax
import jax.numpy as jnp
from jax import lax
from jax.experimental import pallas as pl
from jax.experimental.pallas import tpu as pltpu
from jax.sharding import PartitionSpec as P

PAD = 151643
BLOCK = 64
VMEM = pl.BlockSpec(memory_space=pltpu.VMEM)
HBM = pl.BlockSpec(memory_space=pltpu.HBM)
LAST = (((1,), (1,)), ((), ()))


def project_kernel(
    doc_len, acts_ref, outs_ref, in_ref, out_ref, ids_ref, queries_ref, listing_ref,
    mine_ref, theirs_ref, near_queries_ref, near_listing_ref, acts, outs, infac, outfac, ids, act_sems, out_sems, sems
):
    checkpoints, tokens, _ = acts.shape
    rank = infac.shape[0]
    half = checkpoints * rank
    docs = tokens // doc_len
    blocks = doc_len // BLOCK
    keeps = lax.axis_index("tensor")

    def place(i, first):
        doc = jnp.where(i < first, 0, 1)
        return doc, i - doc * first

    def rows_of(doc, block):
        return pl.ds(pl.multiple_of(doc * doc_len + block * BLOCK, BLOCK), BLOCK)

    def doc_rows(doc):
        return pl.ds(pl.multiple_of(doc * doc_len, doc_len), doc_len)

    def out_copies(doc):
        return [
            pltpu.make_async_copy(outs_ref.at[c, doc_rows(doc)], outs.at[c, doc_rows(doc)], out_sems.at[doc, c])
            for c in range(checkpoints)
        ]

    def act_copies(doc, block):
        at = rows_of(doc, block)
        return [
            pltpu.make_async_copy(acts_ref.at[c, at], acts.at[c, at], act_sems.at[doc * blocks + block, c])
            for c in range(checkpoints)
        ]

    def start(copies):
        for copy in copies:
            copy.start()

    def wait(copies):
        for copy in copies:
            copy.wait()

    out_fac_copy = pltpu.make_async_copy(out_ref, outfac, sems.at[0])
    in_fac_copy = pltpu.make_async_copy(in_ref, infac, sems.at[1])
    ids_copy = pltpu.make_async_copy(ids_ref, ids, sems.at[2])
    late_copies = [
        pltpu.make_async_copy(queries_ref, near_queries_ref, sems.at[3]),
        pltpu.make_async_copy(listing_ref, near_listing_ref, sems.at[4]),
    ]

    ids_copy.start()
    out_fac_copy.start()
    for i in range(docs):
        start(out_copies(i))
    in_fac_copy.start()
    start(act_copies(0, 0))
    ids_copy.wait()
    first, second = (
        sum((ids[doc, block * BLOCK] != PAD).astype(jnp.int32) for block in range(blocks)) for doc in range(docs)
    )

    def start_acts(i, carry):
        start(act_copies(*place(i, first)))
        return carry

    lax.fori_loop(1, first + second, start_acts, 0)
    start(late_copies)

    def put(doc, at, side, found):
        both = jnp.concatenate(found, axis=1)

        @pl.when(doc == keeps)
        def _():
            mine_ref[at, side * half : (side + 1) * half] = both

        @pl.when(doc != keeps)
        def _():
            theirs_ref[at, side * half : (side + 1) * half] = both

    def out_step(doc, carry):
        wait(out_copies(doc))
        found = [
            lax.dot_general(outs[c, doc_rows(doc)], outfac[...], LAST, preferred_element_type=jnp.float32)
            for c in range(checkpoints)
        ]
        put(doc, pl.ds(0, doc_len), 0, found)
        return carry

    def act_step(i, carry):
        doc, block = place(i, first)
        wait(act_copies(doc, block))
        found = [
            lax.dot_general(acts[c, rows_of(doc, block)], infac[...], LAST, preferred_element_type=jnp.float32)
            for c in range(checkpoints)
        ]
        put(doc, pl.ds(pl.multiple_of(block * BLOCK, BLOCK), BLOCK), 1, found)
        return carry

    out_fac_copy.wait()
    lax.fori_loop(0, docs, out_step, 0)
    in_fac_copy.wait()
    lax.fori_loop(0, first + second, act_step, 0)
    wait(late_copies)


def grad_kernel(dp, tensor, checkpoints, ids_ref, mine_ref, other_ref, sent_ref):
    doc_len = mine_ref.shape[0]
    half = mine_ref.shape[1] // 2
    rank = half // checkpoints
    rows = rank // dp
    ids = ids_ref[pl.ds(lax.axis_index("tensor"), 1), :]
    kept = ids != PAD
    places = lax.broadcasted_iota(jnp.int32, ids.shape, 1)
    length = jnp.max(jnp.where(kept, places + 1, 0), axis=1, keepdims=True)
    both = mine_ref[...] + other_ref[...]
    out_side = jnp.where(kept, both[:, :half].T, 0.0)
    in_side = jnp.where(lax.broadcasted_iota(jnp.int32, (doc_len, half), 0) < length, both[:, half:], 0.0)
    sums = jnp.dot(
        out_side, in_side, precision=lax.Precision.HIGHEST, preferred_element_type=jnp.float32
    ) * doc_len ** (-0.5)
    grads = jnp.concatenate(
        [sums[c * rank : (c + 1) * rank, c * rank : (c + 1) * rank] for c in range(checkpoints)], axis=1
    )
    for j in range(dp):
        for k in range(tensor):
            sent_ref[j * tensor + k] = grads[j * rows : (j + 1) * rows]


def score_kernel(dp, checkpoints, terms_ref, queries_ref, listed_ref, sent_ref):
    all_docs, rows, lanes = terms_ref.shape
    rank = lanes // checkpoints
    docs = all_docs // dp
    parts = [terms_ref[:, r, :].astype(jnp.bfloat16) for r in range(rows)]
    part = None
    for c in range(checkpoints):
        grads = jnp.concatenate([p[:, c * rank : (c + 1) * rank] for p in parts], axis=1)
        term = lax.dot_general(grads, queries_ref[c], LAST, preferred_element_type=jnp.float32)
        part = term if part is None else part + term
    part = part * (1.0 / rank)
    places = listed_ref.shape[0]
    every = lax.broadcasted_iota(jnp.int32, part.shape, 0)
    weight = jnp.zeros(part.shape, jnp.float32)
    for k in range(places):
        weight += jnp.where(listed_ref[k : k + 1, :] == every, 1.0 / places, 0.0)
    own = jnp.sum(weight * part, axis=0, keepdims=True)
    for j in range(dp):
        sent_ref[j, 0:docs, :] = part[j * docs : (j + 1) * docs]
        sent_ref[j, docs : docs + 1, :] = own


def total_kernel(parts_ref, scores_ref, listed_ref):
    docs = scores_ref.shape[0]
    total = parts_ref[0]
    for i in range(1, parts_ref.shape[0]):
        total += parts_ref[i]
    scores_ref[...] = total[:docs]
    listed_ref[...] = total[docs:]


def pair_body(dp, tensor, activations, out_grads, proj_in, proj_out, token_ids, queries, query_docs):
    checkpoints, tokens, _ = activations.shape
    rank = proj_in.shape[1]
    docs, doc_len = token_ids.shape
    rows = rank // dp
    own_queries = queries.shape[1]
    lanes = checkpoints * rank
    steps = tokens // BLOCK
    wide = activations.size + out_grads.size
    f32 = jnp.float32

    near = (activations, out_grads, proj_in.T, proj_out.T, token_ids, queries, query_docs.T)
    mine, theirs, near_queries, near_listing = pl.pallas_call(
        functools.partial(project_kernel, doc_len),
        in_specs=[HBM] * 7,
        out_specs=[VMEM] * 4,
        out_shape=[
            pltpu.VMEM((doc_len, 2 * lanes), f32),
            pltpu.VMEM((doc_len, 2 * lanes), f32),
            pltpu.VMEM(queries.shape, queries.dtype),
            pltpu.VMEM(query_docs.shape[::-1], query_docs.dtype),
        ],
        scratch_shapes=[
            pltpu.VMEM(activations.shape, activations.dtype),
            pltpu.VMEM(out_grads.shape, out_grads.dtype),
            pltpu.VMEM(proj_in.shape[::-1], proj_in.dtype),
            pltpu.VMEM(proj_out.shape[::-1], proj_out.dtype),
            pltpu.SMEM(token_ids.shape, token_ids.dtype),
            pltpu.SemaphoreType.DMA((steps, checkpoints)),
            pltpu.SemaphoreType.DMA((docs, checkpoints)),
            pltpu.SemaphoreType.DMA((5,)),
        ],
        compiler_params=pltpu.CompilerParams(vmem_limit_bytes=44 << 20),
        cost_estimate=pl.CostEstimate(flops=2 * wide * rank, bytes_accessed=2 * wide, transcendentals=0),
        name="project",
    )(*(pltpu.with_memory_space_constraint(x, pltpu.HBM) for x in near))
    other = lax.ppermute(theirs, "tensor", [(0, 1), (1, 0)])
    sent = pl.pallas_call(
        functools.partial(grad_kernel, dp, tensor, checkpoints),
        in_specs=[VMEM] * 3,
        out_specs=VMEM,
        out_shape=jax.ShapeDtypeStruct((dp * tensor, rows, lanes), f32),
        compiler_params=pltpu.CompilerParams(vmem_limit_bytes=4 << 20),
        name="doc_grads",
    )(token_ids, mine, other)
    terms = lax.all_to_all(sent, ("dp", "tensor"), 0, 0, tiled=True)
    parts = pl.pallas_call(
        functools.partial(score_kernel, dp, checkpoints),
        in_specs=[VMEM] * 3,
        out_specs=VMEM,
        out_shape=jax.ShapeDtypeStruct((dp, docs + 1, own_queries), f32),
        compiler_params=pltpu.CompilerParams(vmem_limit_bytes=8 << 20),
        name="partial_scores",
    )(terms, near_queries, near_listing)
    parts = lax.all_to_all(parts, "dp", 0, 0, tiled=True)
    scores, listed = pl.pallas_call(
        total_kernel,
        in_specs=[VMEM],
        out_specs=[VMEM] * 2,
        out_shape=[jax.ShapeDtypeStruct((docs, own_queries), f32), jax.ShapeDtypeStruct((1, own_queries), f32)],
        compiler_params=pltpu.CompilerParams(vmem_limit_bytes=4 << 20),
        name="totals",
    )(parts)
    return scores, listed.reshape(own_queries)


def sum_over_tensor(part, size):
    if size == 2:
        return part + lax.ppermute(part, "tensor", [(0, 1), (1, 0)])
    return lax.psum(part, "tensor")


def any_body(dp, tensor, activations, out_grads, proj_in, proj_out, token_ids, queries, query_docs):
    checkpoints = activations.shape[0]
    rank = proj_in.shape[1]
    docs, doc_len = token_ids.shape
    rows = rank // dp
    own_queries = queries.shape[1]

    out_part = jnp.einsum("ctd,dr->ctr", out_grads, proj_out, preferred_element_type=jnp.float32)
    out_proj = sum_over_tensor(out_part, tensor)
    in_part = jnp.einsum("ctf,fr->ctr", activations, proj_in, preferred_element_type=jnp.float32)
    keep = (token_ids != PAD).astype(jnp.float32).reshape(1, docs, doc_len, 1)
    out_proj = out_proj.reshape(checkpoints, docs, doc_len, rank) * keep
    in_part = in_part.reshape(checkpoints, docs, doc_len, rank)
    term = jnp.einsum("cntr,cnts->crns", out_proj, in_part, precision=lax.Precision.HIGHEST)
    term = term.reshape(checkpoints, dp, 1, rows, docs * rank).transpose(1, 2, 0, 3, 4)
    term = jnp.broadcast_to(term, (dp, tensor, checkpoints, rows, docs * rank))
    term = term.reshape(dp * tensor, checkpoints, rows, docs * rank)
    terms = lax.all_to_all(term, ("dp", "tensor"), 0, 0, tiled=True)
    grads = terms.reshape(dp, tensor, checkpoints, rows, docs, rank).sum(1) * doc_len ** (-0.5)
    grads = grads.astype(jnp.bfloat16).transpose(1, 0, 3, 2, 4).reshape(checkpoints, dp * docs, rows * rank)

    part = jnp.einsum("cnf,cqf->nq", grads, queries, preferred_element_type=jnp.float32)
    every_doc = jnp.arange(dp * docs, dtype=jnp.int32)
    listing = (query_docs.T[None] == every_doc[:, None, None]).sum(1).astype(jnp.float32)
    listed_part = (listing * part).sum(0)
    sent = jnp.concatenate(
        [
            part.reshape(dp, docs, own_queries),
            jnp.broadcast_to(listed_part, (dp, 1, own_queries)),
        ],
        axis=1,
    )
    total = lax.all_to_all(sent, "dp", 0, 0, tiled=True).sum(0) / rank
    return total[:docs], total[docs] / query_docs.shape[1]


def solution(mesh):
    dp, tensor = mesh.shape["dp"], mesh.shape["tensor"]

    def body(*arrays):
        docs, doc_len = arrays[4].shape
        paired = tensor == 2 and docs == 2 and doc_len % BLOCK == 0
        return (pair_body if paired else any_body)(dp, tensor, *arrays)

    in_specs = (
        P(None, ("parts", "dp"), "tensor"),
        P(None, ("parts", "dp"), "tensor"),
        P("tensor", None),
        P("tensor", None),
        P(("parts", "dp"), None),
        P(None, "tensor", "dp"),
        P(("parts", "tensor"), None),
    )
    out_specs = (P(("parts", "dp"), "tensor"), P(("parts", "tensor")))
    return jax.shard_map(
        body,
        mesh=mesh,
        in_specs=in_specs,
        out_specs=out_specs,
        check_vma=False,
    )
```

```python
import functools

import jax
import jax.numpy as jnp
from jax import lax
from jax.experimental import pallas as pl
from jax.experimental.pallas import tpu as pltpu
from jax.sharding import PartitionSpec as P

PAD = 151643
BLOCK = 64
VMEM = pl.BlockSpec(memory_space=pltpu.VMEM)
HBM = pl.BlockSpec(memory_space=pltpu.HBM)
LAST = (((1,), (1,)), ((), ()))


def project_kernel(
    doc_len, acts_ref, outs_ref, in_ref, out_ref, ids_ref, queries_ref, listing_ref,
    mine_ref, theirs_ref, near_queries_ref, near_listing_ref, acts, outs, infac, outfac, ids, act_sems, out_sems, sems
):
    checkpoints, tokens, _ = acts_ref.shape
    docs = tokens // doc_len
    blocks = doc_len // BLOCK
    keeps = lax.axis_index("tensor")

    def place(i, first):
        doc = jnp.where(i < first, 0, 1)
        return doc, i - doc * first

    def rows_of(doc, block):
        return pl.ds(pl.multiple_of(doc * doc_len + block * BLOCK, BLOCK), BLOCK)

    def copies_of(doc, block, wide_ref, wide, wide_sems):
        slot = doc * blocks + block
        return [
            pltpu.make_async_copy(
                wide_ref.at[c, rows_of(doc, block)], wide.at[slot, pl.ds(c * BLOCK, BLOCK)], wide_sems.at[slot, c]
            )
            for c in range(checkpoints)
        ]

    def out_copies(doc, block):
        return copies_of(doc, block, outs_ref, outs, out_sems)

    def act_copies(doc, block):
        return copies_of(doc, block, acts_ref, acts, act_sems)

    def start(copies):
        for copy in copies:
            copy.start()

    def wait(copies):
        for copy in copies:
            copy.wait()

    out_fac_copy = pltpu.make_async_copy(out_ref, outfac, sems.at[0])
    in_fac_copy = pltpu.make_async_copy(in_ref, infac, sems.at[1])
    ids_copy = pltpu.make_async_copy(ids_ref, ids, sems.at[2])
    late_copies = [
        pltpu.make_async_copy(queries_ref, near_queries_ref, sems.at[3]),
        pltpu.make_async_copy(listing_ref, near_listing_ref, sems.at[4]),
    ]

    ids_copy.start()
    out_fac_copy.start()
    start(out_copies(0, 0))
    in_fac_copy.start()
    start(act_copies(0, 0))
    ids_copy.wait()
    first, second = (
        sum((ids[doc, block * BLOCK] != PAD).astype(jnp.int32) for block in range(blocks)) for doc in range(docs)
    )

    def start_acts(i, carry):
        start(out_copies(*place(i, first)))
        start(act_copies(*place(i, first)))
        return carry

    lax.fori_loop(1, first + second, start_acts, 0)
    start(late_copies)

    mine_ref[...] = jnp.zeros_like(mine_ref)
    theirs_ref[...] = jnp.zeros_like(theirs_ref)

    def step(i, carry):
        doc, block = place(i, first)
        slot = doc * blocks + block
        wait(out_copies(doc, block))
        wait(act_copies(doc, block))
        found = [
            lax.dot_general(wide[slot], factor[...], LAST, preferred_element_type=jnp.float32)
            for wide, factor in ((outs, outfac), (acts, infac))
        ]
        line = jnp.concatenate([x[c * BLOCK : (c + 1) * BLOCK] for x in found for c in range(checkpoints)], axis=1)
        at = pl.ds(pl.multiple_of(block * BLOCK, BLOCK), BLOCK)

        @pl.when(doc == keeps)
        def _():
            mine_ref[at] = line

        @pl.when(doc != keeps)
        def _():
            theirs_ref[at] = line

        return carry

    out_fac_copy.wait()
    in_fac_copy.wait()
    lax.fori_loop(0, first + second, step, 0)
    wait(late_copies)


def grad_kernel(dp, tensor, checkpoints, ids_ref, mine_ref, other_ref, sent_ref):
    doc_len = mine_ref.shape[0]
    half = mine_ref.shape[1] // 2
    rank = half // checkpoints
    rows = rank // dp
    ids = ids_ref[pl.ds(lax.axis_index("tensor"), 1), :]
    keep = jnp.where(ids != PAD, doc_len**-0.5, 0.0)
    both = mine_ref[...] + other_ref[...]
    sums = jnp.dot(
        both[:, :half].T * keep,
        both[:, half:],
        precision=lax.Precision.HIGHEST,
        preferred_element_type=jnp.float32,
    )
    grads = jnp.concatenate(
        [sums[c * rank : (c + 1) * rank, c * rank : (c + 1) * rank] for c in range(checkpoints)], axis=1
    )
    for j in range(dp):
        for k in range(tensor):
            sent_ref[j * tensor + k] = grads[j * rows : (j + 1) * rows]


def score_kernel(dp, checkpoints, terms_ref, queries_ref, listed_ref, sent_ref):
    all_docs, rows, lanes = terms_ref.shape
    rank = lanes // checkpoints
    docs = all_docs // dp
    parts = [terms_ref[:, r, :].astype(jnp.bfloat16) for r in range(rows)]
    part = None
    for c in range(checkpoints):
        grads = jnp.concatenate([p[:, c * rank : (c + 1) * rank] for p in parts], axis=1)
        term = lax.dot_general(grads, queries_ref[c], LAST, preferred_element_type=jnp.float32)
        part = term if part is None else part + term
    part = part * (1.0 / rank)
    places = listed_ref.shape[0]
    every = lax.broadcasted_iota(jnp.int32, part.shape, 0)
    weight = jnp.zeros(part.shape, jnp.float32)
    for k in range(places):
        weight += jnp.where(listed_ref[k : k + 1, :] == every, 1.0 / places, 0.0)
    own = jnp.sum(weight * part, axis=0, keepdims=True)
    lines = part.shape[1] // 128
    for line in range(lines):
        at = slice(line * 128, (line + 1) * 128)
        for j in range(dp):
            for doc in range(docs):
                n = j * docs + doc
                sent_ref[j, pl.ds(doc * lines + line, 1), :] = part[n : n + 1, at]
            sent_ref[j, pl.ds(docs * lines + line, 1), :] = own[:, at]


def total_kernel(parts_ref, scores_ref, listed_ref):
    docs, columns = scores_ref.shape
    lines = columns // 128
    total = parts_ref[0]
    for i in range(1, parts_ref.shape[0]):
        total += parts_ref[i]
    for line in range(lines):
        at = slice(line * 128, (line + 1) * 128)
        for doc in range(docs):
            n = doc * lines + line
            scores_ref[doc : doc + 1, at] = total[n : n + 1]
        n = docs * lines + line
        listed_ref[:, at] = total[n : n + 1]


def pair_body(dp, tensor, activations, out_grads, proj_in, proj_out, token_ids, queries, query_docs):
    checkpoints, tokens, _ = activations.shape
    rank = proj_in.shape[1]
    docs, doc_len = token_ids.shape
    rows = rank // dp
    own_queries = queries.shape[1]
    lanes = checkpoints * rank
    steps = tokens // BLOCK
    wide = activations.size + out_grads.size
    f32 = jnp.float32

    near = (activations, out_grads, proj_in.T, proj_out.T, token_ids, queries, query_docs.T)
    mine, theirs, near_queries, near_listing = pl.pallas_call(
        functools.partial(project_kernel, doc_len),
        in_specs=[HBM] * 7,
        out_specs=[VMEM] * 4,
        out_shape=[
            pltpu.VMEM((doc_len, 2 * lanes), f32),
            pltpu.VMEM((doc_len, 2 * lanes), f32),
            pltpu.VMEM(queries.shape, queries.dtype),
            pltpu.VMEM(query_docs.shape[::-1], query_docs.dtype),
        ],
        scratch_shapes=[
            pltpu.VMEM((tokens // BLOCK, checkpoints * BLOCK, activations.shape[2]), activations.dtype),
            pltpu.VMEM((tokens // BLOCK, checkpoints * BLOCK, out_grads.shape[2]), out_grads.dtype),
            pltpu.VMEM(proj_in.shape[::-1], proj_in.dtype),
            pltpu.VMEM(proj_out.shape[::-1], proj_out.dtype),
            pltpu.SMEM(token_ids.shape, token_ids.dtype),
            pltpu.SemaphoreType.DMA((steps, checkpoints)),
            pltpu.SemaphoreType.DMA((steps, checkpoints)),
            pltpu.SemaphoreType.DMA((5,)),
        ],
        compiler_params=pltpu.CompilerParams(vmem_limit_bytes=44 << 20),
        cost_estimate=pl.CostEstimate(flops=2 * wide * rank, bytes_accessed=2 * wide, transcendentals=0),
        name="project",
    )(*(pltpu.with_memory_space_constraint(x, pltpu.HBM) for x in near))
    other = lax.ppermute(theirs, "tensor", [(0, 1), (1, 0)])
    sent = pl.pallas_call(
        functools.partial(grad_kernel, dp, tensor, checkpoints),
        in_specs=[VMEM] * 3,
        out_specs=VMEM,
        out_shape=jax.ShapeDtypeStruct((dp * tensor, rows, lanes), f32),
        compiler_params=pltpu.CompilerParams(vmem_limit_bytes=4 << 20),
        name="doc_grads",
    )(token_ids, mine, other)
    terms = lax.all_to_all(sent, ("dp", "tensor"), 0, 0, tiled=True)
    parts = pl.pallas_call(
        functools.partial(score_kernel, dp, checkpoints),
        in_specs=[VMEM] * 3,
        out_specs=VMEM,
        out_shape=jax.ShapeDtypeStruct((dp, (docs + 1) * own_queries // 128, 128), f32),
        compiler_params=pltpu.CompilerParams(vmem_limit_bytes=8 << 20),
        name="partial_scores",
    )(terms, near_queries, near_listing)
    parts = lax.all_to_all(parts, "dp", 0, 0, tiled=True)
    scores, listed = pl.pallas_call(
        total_kernel,
        in_specs=[VMEM],
        out_specs=[VMEM] * 2,
        out_shape=[jax.ShapeDtypeStruct((docs, own_queries), f32), jax.ShapeDtypeStruct((1, own_queries), f32)],
        compiler_params=pltpu.CompilerParams(vmem_limit_bytes=4 << 20),
        name="totals",
    )(parts)
    return scores, listed.reshape(own_queries)


def sum_over_tensor(part, size):
    if size == 2:
        return part + lax.ppermute(part, "tensor", [(0, 1), (1, 0)])
    return lax.psum(part, "tensor")


def any_body(dp, tensor, activations, out_grads, proj_in, proj_out, token_ids, queries, query_docs):
    checkpoints = activations.shape[0]
    rank = proj_in.shape[1]
    docs, doc_len = token_ids.shape
    rows = rank // dp
    own_queries = queries.shape[1]

    out_part = jnp.einsum("ctd,dr->ctr", out_grads, proj_out, preferred_element_type=jnp.float32)
    out_proj = sum_over_tensor(out_part, tensor)
    in_part = jnp.einsum("ctf,fr->ctr", activations, proj_in, preferred_element_type=jnp.float32)
    keep = (token_ids != PAD).astype(jnp.float32).reshape(1, docs, doc_len, 1)
    out_proj = out_proj.reshape(checkpoints, docs, doc_len, rank) * keep
    in_part = in_part.reshape(checkpoints, docs, doc_len, rank)
    term = jnp.einsum("cntr,cnts->crns", out_proj, in_part, precision=lax.Precision.HIGHEST)
    term = term.reshape(checkpoints, dp, 1, rows, docs * rank).transpose(1, 2, 0, 3, 4)
    term = jnp.broadcast_to(term, (dp, tensor, checkpoints, rows, docs * rank))
    term = term.reshape(dp * tensor, checkpoints, rows, docs * rank)
    terms = lax.all_to_all(term, ("dp", "tensor"), 0, 0, tiled=True)
    grads = terms.reshape(dp, tensor, checkpoints, rows, docs, rank).sum(1) * doc_len ** (-0.5)
    grads = grads.astype(jnp.bfloat16).transpose(1, 0, 3, 2, 4).reshape(checkpoints, dp * docs, rows * rank)

    part = jnp.einsum("cnf,cqf->nq", grads, queries, preferred_element_type=jnp.float32)
    every_doc = jnp.arange(dp * docs, dtype=jnp.int32)
    listing = (query_docs.T[None] == every_doc[:, None, None]).sum(1).astype(jnp.float32)
    listed_part = (listing * part).sum(0)
    sent = jnp.concatenate(
        [
            part.reshape(dp, docs, own_queries),
            jnp.broadcast_to(listed_part, (dp, 1, own_queries)),
        ],
        axis=1,
    )
    total = lax.all_to_all(sent, "dp", 0, 0, tiled=True).sum(0) / rank
    return total[:docs], total[docs] / query_docs.shape[1]


def solution(mesh):
    dp, tensor = mesh.shape["dp"], mesh.shape["tensor"]

    def body(*arrays):
        docs, doc_len = arrays[4].shape
        paired = tensor == 2 and docs == 2 and doc_len % BLOCK == 0 and arrays[5].shape[1] % 128 == 0
        return (pair_body if paired else any_body)(dp, tensor, *arrays)

    in_specs = (
        P(None, ("parts", "dp"), "tensor"),
        P(None, ("parts", "dp"), "tensor"),
        P("tensor", None),
        P("tensor", None),
        P(("parts", "dp"), None),
        P(None, "tensor", "dp"),
        P(("parts", "tensor"), None),
    )
    out_specs = (P(("parts", "dp"), "tensor"), P(("parts", "tensor")))
    return jax.shard_map(
        body,
        mesh=mesh,
        in_specs=in_specs,
        out_specs=out_specs,
        check_vma=False,
    )
```

```python
import functools

import jax
import jax.numpy as jnp
from jax import lax
from jax.experimental import pallas as pl
from jax.experimental.pallas import tpu as pltpu
from jax.sharding import PartitionSpec as P

PAD = 151643
BLOCK = 64
VMEM = pl.BlockSpec(memory_space=pltpu.VMEM)
HBM = pl.BlockSpec(memory_space=pltpu.HBM)
LAST = (((1,), (1,)), ((), ()))


def project_kernel(
    doc_len, acts_ref, outs_ref, in_ref, out_ref, ids_ref, queries_ref, listing_ref,
    mine_ref, theirs_ref, near_queries_ref, near_listing_ref, wide, factor, ids, wide_sems, sems
):
    checkpoints, tokens, in_width = acts_ref.shape
    rank, out_width = out_ref.shape
    docs = tokens // doc_len
    blocks = doc_len // BLOCK
    keeps = lax.axis_index("tensor")
    in_cut, out_cut = pl.ds(0, in_width), pl.ds(in_width, out_width)

    def place(i, first):
        doc = jnp.where(i < first, 0, 1)
        return doc, i - doc * first

    def block_copies(doc, block):
        slot = doc * blocks + block
        rows = pl.ds(pl.multiple_of(doc * doc_len + block * BLOCK, BLOCK), BLOCK)
        return [
            pltpu.make_async_copy(
                source.at[c, rows], wide.at[slot, pl.ds(c * BLOCK, BLOCK), cut], wide_sems.at[slot, c, side]
            )
            for c in range(checkpoints)
            for side, (source, cut) in enumerate(((acts_ref, in_cut), (outs_ref, out_cut)))
        ]

    def start(copies):
        for copy in copies:
            copy.start()

    def wait(copies):
        for copy in copies:
            copy.wait()

    ids_copy = pltpu.make_async_copy(ids_ref, ids, sems.at[0])
    factor_copies = [
        pltpu.make_async_copy(in_ref, factor.at[pl.ds(0, rank), in_cut], sems.at[1]),
        pltpu.make_async_copy(out_ref, factor.at[pl.ds(rank, rank), out_cut], sems.at[2]),
    ]
    late_copies = [
        pltpu.make_async_copy(queries_ref, near_queries_ref, sems.at[3]),
        pltpu.make_async_copy(listing_ref, near_listing_ref, sems.at[4]),
    ]

    ids_copy.start()
    start(factor_copies)
    start(block_copies(0, 0))
    factor[:rank, in_width:] = jnp.zeros((rank, out_width), factor.dtype)
    factor[rank:, :in_width] = jnp.zeros((rank, in_width), factor.dtype)
    ids_copy.wait()
    first, second = (
        sum((ids[doc, block * BLOCK] != PAD).astype(jnp.int32) for block in range(blocks)) for doc in range(docs)
    )

    def start_block(i, carry):
        start(block_copies(*place(i, first)))
        return carry

    lax.fori_loop(1, first + second, start_block, 0)
    start(late_copies)

    mine_ref[...] = jnp.zeros_like(mine_ref)
    theirs_ref[...] = jnp.zeros_like(theirs_ref)

    def step(i, carry):
        doc, block = place(i, first)
        wait(block_copies(doc, block))
        found = lax.dot_general(
            wide[doc * blocks + block], factor[...], LAST, preferred_element_type=jnp.float32
        )
        line = jnp.concatenate([found[c * BLOCK : (c + 1) * BLOCK] for c in range(checkpoints)], axis=1)
        at = pl.ds(pl.multiple_of(block * BLOCK, BLOCK), BLOCK)

        @pl.when(doc == keeps)
        def _():
            mine_ref[at] = line

        @pl.when(doc != keeps)
        def _():
            theirs_ref[at] = line

        return carry

    wait(factor_copies)
    lax.fori_loop(0, first + second, step, 0)
    wait(late_copies)


def grad_kernel(dp, tensor, checkpoints, ids_ref, mine_ref, other_ref, sent_ref):
    doc_len, lanes = mine_ref.shape
    pair = lanes // checkpoints
    rank = pair // 2
    rows = rank // dp
    ids = ids_ref[pl.ds(lax.axis_index("tensor"), 1), :]
    keep = jnp.where(ids != PAD, doc_len**-0.5, 0.0)
    sides = mine_ref[...] + other_ref[...]
    in_side, out_side = (
        jnp.concatenate([sides[:, c * pair + at : c * pair + at + rank] for c in range(checkpoints)], axis=1)
        for at in (0, rank)
    )
    sums = jnp.dot(
        out_side.T * keep, in_side, precision=lax.Precision.HIGHEST, preferred_element_type=jnp.float32
    )
    grads = jnp.concatenate(
        [sums[c * rank : (c + 1) * rank, c * rank : (c + 1) * rank] for c in range(checkpoints)], axis=1
    )
    for j in range(dp):
        for k in range(tensor):
            sent_ref[j * tensor + k] = grads[j * rows : (j + 1) * rows].astype(sent_ref.dtype)


def score_kernel(dp, checkpoints, terms_ref, queries_ref, listed_ref, sent_ref):
    all_docs, rows, lanes = terms_ref.shape
    rank = lanes // checkpoints
    docs = all_docs // dp
    terms = terms_ref[...].astype(jnp.float32)
    parts = [terms[:, r, :].astype(jnp.bfloat16) for r in range(rows)]
    part = None
    for c in range(checkpoints):
        grads = jnp.concatenate([p[:, c * rank : (c + 1) * rank] for p in parts], axis=1)
        term = lax.dot_general(grads, queries_ref[c], LAST, preferred_element_type=jnp.float32)
        part = term if part is None else part + term
    part = part * (1.0 / rank)
    places = listed_ref.shape[0]
    every = lax.broadcasted_iota(jnp.int32, part.shape, 0)
    weight = jnp.zeros(part.shape, jnp.float32)
    for k in range(places):
        weight += jnp.where(listed_ref[k : k + 1, :] == every, 1.0 / places, 0.0)
    own = jnp.sum(weight * part, axis=0, keepdims=True)
    lines = part.shape[1] // 128
    for line in range(lines):
        at = slice(line * 128, (line + 1) * 128)
        for j in range(dp):
            for doc in range(docs):
                n = j * docs + doc
                sent_ref[j, pl.ds(doc * lines + line, 1), :] = part[n : n + 1, at]
            sent_ref[j, pl.ds(docs * lines + line, 1), :] = own[:, at]


def total_kernel(parts_ref, scores_ref, listed_ref):
    docs, columns = scores_ref.shape
    lines = columns // 128
    total = parts_ref[0]
    for i in range(1, parts_ref.shape[0]):
        total += parts_ref[i]
    for line in range(lines):
        at = slice(line * 128, (line + 1) * 128)
        for doc in range(docs):
            n = doc * lines + line
            scores_ref[doc : doc + 1, at] = total[n : n + 1]
        n = docs * lines + line
        listed_ref[:, at] = total[n : n + 1]


def pair_body(dp, tensor, activations, out_grads, proj_in, proj_out, token_ids, queries, query_docs):
    checkpoints, tokens, _ = activations.shape
    rank = proj_in.shape[1]
    docs, doc_len = token_ids.shape
    rows = rank // dp
    own_queries = queries.shape[1]
    lanes = checkpoints * rank
    wide = activations.size + out_grads.size
    width = activations.shape[2] + out_grads.shape[2]
    f32 = jnp.float32

    near = (activations, out_grads, proj_in.T, proj_out.T, token_ids, queries, query_docs.T)
    mine, theirs, near_queries, near_listing = pl.pallas_call(
        functools.partial(project_kernel, doc_len),
        in_specs=[HBM] * 7,
        out_specs=[VMEM] * 4,
        out_shape=[
            pltpu.VMEM((doc_len, 2 * lanes), f32),
            pltpu.VMEM((doc_len, 2 * lanes), f32),
            pltpu.VMEM(queries.shape, queries.dtype),
            pltpu.VMEM(query_docs.shape[::-1], query_docs.dtype),
        ],
        scratch_shapes=[
            pltpu.VMEM((tokens // BLOCK, checkpoints * BLOCK, width), activations.dtype),
            pltpu.VMEM((2 * rank, width), proj_in.dtype),
            pltpu.SMEM(token_ids.shape, token_ids.dtype),
            pltpu.SemaphoreType.DMA((tokens // BLOCK, checkpoints, 2)),
            pltpu.SemaphoreType.DMA((5,)),
        ],
        compiler_params=pltpu.CompilerParams(vmem_limit_bytes=44 << 20),
        cost_estimate=pl.CostEstimate(flops=2 * wide * rank, bytes_accessed=2 * wide, transcendentals=0),
        name="project",
    )(*(pltpu.with_memory_space_constraint(x, pltpu.HBM) for x in near))
    other = lax.ppermute(theirs, "tensor", [(0, 1), (1, 0)])
    sent = pl.pallas_call(
        functools.partial(grad_kernel, dp, tensor, checkpoints),
        in_specs=[VMEM] * 3,
        out_specs=VMEM,
        out_shape=jax.ShapeDtypeStruct((dp * tensor, rows, lanes), jnp.bfloat16),
        compiler_params=pltpu.CompilerParams(vmem_limit_bytes=4 << 20),
        name="doc_grads",
    )(token_ids, mine, other)
    terms = lax.all_to_all(sent, ("dp", "tensor"), 0, 0, tiled=True)
    parts = pl.pallas_call(
        functools.partial(score_kernel, dp, checkpoints),
        in_specs=[VMEM] * 3,
        out_specs=VMEM,
        out_shape=jax.ShapeDtypeStruct((dp, (docs + 1) * own_queries // 128, 128), f32),
        compiler_params=pltpu.CompilerParams(vmem_limit_bytes=8 << 20),
        name="partial_scores",
    )(terms, near_queries, near_listing)
    parts = lax.all_to_all(parts, "dp", 0, 0, tiled=True)
    scores, listed = pl.pallas_call(
        total_kernel,
        in_specs=[VMEM],
        out_specs=[VMEM] * 2,
        out_shape=[jax.ShapeDtypeStruct((docs, own_queries), f32), jax.ShapeDtypeStruct((1, own_queries), f32)],
        compiler_params=pltpu.CompilerParams(vmem_limit_bytes=4 << 20),
        name="totals",
    )(parts)
    return scores, listed.reshape(own_queries)


def sum_over_tensor(part, size):
    if size == 2:
        return part + lax.ppermute(part, "tensor", [(0, 1), (1, 0)])
    return lax.psum(part, "tensor")


def any_body(dp, tensor, activations, out_grads, proj_in, proj_out, token_ids, queries, query_docs):
    checkpoints = activations.shape[0]
    rank = proj_in.shape[1]
    docs, doc_len = token_ids.shape
    rows = rank // dp
    own_queries = queries.shape[1]

    out_part = jnp.einsum("ctd,dr->ctr", out_grads, proj_out, preferred_element_type=jnp.float32)
    out_proj = sum_over_tensor(out_part, tensor)
    in_part = jnp.einsum("ctf,fr->ctr", activations, proj_in, preferred_element_type=jnp.float32)
    keep = (token_ids != PAD).astype(jnp.float32).reshape(1, docs, doc_len, 1)
    out_proj = out_proj.reshape(checkpoints, docs, doc_len, rank) * keep
    in_part = in_part.reshape(checkpoints, docs, doc_len, rank)
    term = jnp.einsum("cntr,cnts->crns", out_proj, in_part, precision=lax.Precision.HIGHEST)
    term = term.reshape(checkpoints, dp, 1, rows, docs * rank).transpose(1, 2, 0, 3, 4)
    term = jnp.broadcast_to(term, (dp, tensor, checkpoints, rows, docs * rank))
    term = term.reshape(dp * tensor, checkpoints, rows, docs * rank)
    terms = lax.all_to_all(term, ("dp", "tensor"), 0, 0, tiled=True)
    grads = terms.reshape(dp, tensor, checkpoints, rows, docs, rank).sum(1) * doc_len ** (-0.5)
    grads = grads.astype(jnp.bfloat16).transpose(1, 0, 3, 2, 4).reshape(checkpoints, dp * docs, rows * rank)

    part = jnp.einsum("cnf,cqf->nq", grads, queries, preferred_element_type=jnp.float32)
    every_doc = jnp.arange(dp * docs, dtype=jnp.int32)
    listing = (query_docs.T[None] == every_doc[:, None, None]).sum(1).astype(jnp.float32)
    listed_part = (listing * part).sum(0)
    sent = jnp.concatenate(
        [
            part.reshape(dp, docs, own_queries),
            jnp.broadcast_to(listed_part, (dp, 1, own_queries)),
        ],
        axis=1,
    )
    total = lax.all_to_all(sent, "dp", 0, 0, tiled=True).sum(0) / rank
    return total[:docs], total[docs] / query_docs.shape[1]


def solution(mesh):
    dp, tensor = mesh.shape["dp"], mesh.shape["tensor"]

    def body(*arrays):
        docs, doc_len = arrays[4].shape
        whole_tiles = all(n % 128 == 0 for n in (arrays[0].shape[2], arrays[1].shape[2], arrays[5].shape[1]))
        paired = tensor == 2 and docs == 2 and doc_len % BLOCK == 0 and whole_tiles
        return (pair_body if paired else any_body)(dp, tensor, *arrays)

    in_specs = (
        P(None, ("parts", "dp"), "tensor"),
        P(None, ("parts", "dp"), "tensor"),
        P("tensor", None),
        P("tensor", None),
        P(("parts", "dp"), None),
        P(None, "tensor", "dp"),
        P(("parts", "tensor"), None),
    )
    out_specs = (P(("parts", "dp"), "tensor"), P(("parts", "tensor")))
    return jax.shard_map(
        body,
        mesh=mesh,
        in_specs=in_specs,
        out_specs=out_specs,
        check_vma=False,
    )
```

```python
import functools

import jax
import jax.numpy as jnp
from jax import lax
from jax.experimental import pallas as pl
from jax.experimental.pallas import tpu as pltpu
from jax.sharding import PartitionSpec as P

PAD = 151643
BLOCK = 32
STEP = 2
VMEM = pl.BlockSpec(memory_space=pltpu.VMEM)
HBM = pl.BlockSpec(memory_space=pltpu.HBM)
LAST = (((1,), (1,)), ((), ()))


def project_kernel(
    doc_len, acts_ref, outs_ref, in_ref, out_ref, ids_ref, queries_ref, listing_ref,
    mine_ref, theirs_ref, near_queries_ref, near_listing_ref, wide, factor, found_both, ids, wide_sems, sems
):
    checkpoints, tokens, in_width = acts_ref.shape
    rank, out_width = out_ref.shape
    docs = tokens // doc_len
    blocks = doc_len // BLOCK
    keeps = lax.axis_index("tensor")
    in_cut, out_cut = pl.ds(0, in_width), pl.ds(in_width, out_width)

    def place(i, first):
        doc = jnp.where(i < first, 0, 1)
        return doc, i - doc * first

    def block_copies(slot, doc, block):
        rows = pl.ds(pl.multiple_of(doc * doc_len + block * BLOCK, BLOCK), BLOCK)
        return [
            pltpu.make_async_copy(source.at[:, rows], wide.at[slot, :, :, cut], wide_sems.at[slot])
            for source, cut in ((acts_ref, in_cut), (outs_ref, out_cut))
        ]

    def start(copies):
        for copy in copies:
            copy.start()

    def wait(copies):
        for copy in copies:
            copy.wait()

    ids_copy = pltpu.make_async_copy(ids_ref, ids, sems.at[0])
    factor_copies = [
        pltpu.make_async_copy(in_ref, factor.at[pl.ds(0, rank), in_cut], sems.at[1]),
        pltpu.make_async_copy(out_ref, factor.at[pl.ds(rank, rank), out_cut], sems.at[2]),
    ]
    late_copies = [
        pltpu.make_async_copy(queries_ref, near_queries_ref, sems.at[3]),
        pltpu.make_async_copy(listing_ref, near_listing_ref, sems.at[4]),
    ]

    ids_copy.start()
    start(factor_copies)
    for block in range(STEP):
        start(block_copies(block, 0, block))
    factor[:rank, in_width:] = jnp.zeros((rank, out_width), factor.dtype)
    factor[rank:, :in_width] = jnp.zeros((rank, in_width), factor.dtype)
    ids_copy.wait()
    first, second = (
        sum((ids[doc, block * BLOCK] != PAD).astype(jnp.int32) for block in range(blocks)) for doc in range(docs)
    )

    total = first + second

    def start_block(i, carry):
        start(block_copies(i, *place(i, first)))
        return carry

    lax.fori_loop(STEP, total, start_block, 0)
    start(late_copies)

    found_both[...] = jnp.zeros_like(found_both)

    def put(i, found):
        doc, block = place(i, first)
        line = jnp.concatenate([found[c * BLOCK : (c + 1) * BLOCK] for c in range(checkpoints)], axis=1)
        at = pl.ds(pl.multiple_of(block * BLOCK, BLOCK), BLOCK)

        found_both[jnp.where(doc == keeps, 0, 1), at] = line

    def wait_block(i):
        pltpu.make_async_copy(wide.at[i], wide.at[i], wide_sems.at[i]).wait()

    def step(j, carry):
        slots = pl.ds(j * STEP, STEP)
        wait_block(j * STEP)
        for i in range(1, STEP):
            pl.when(j * STEP + i < total)(lambda i=i: wait_block(j * STEP + i))
        rows = checkpoints * BLOCK
        found = lax.dot_general(
            wide[slots].reshape(STEP * rows, in_width + out_width),
            factor[...],
            LAST,
            preferred_element_type=jnp.float32,
        )
        put(j * STEP, found[:rows])
        for i in range(1, STEP):
            pl.when(j * STEP + i < total)(lambda i=i: put(j * STEP + i, found[i * rows : (i + 1) * rows]))
        return carry

    wait(factor_copies)
    lax.fori_loop(0, (total + STEP - 1) // STEP, step, 0)
    mine_ref[...] = found_both[0]
    theirs_ref[...] = found_both[1]
    wait(late_copies)


def grad_kernel(dp, tensor, checkpoints, ids_ref, mine_ref, other_ref, sent_ref):
    doc_len, lanes = mine_ref.shape
    pair = lanes // checkpoints
    rank = pair // 2
    rows = rank // dp
    ids = ids_ref[pl.ds(lax.axis_index("tensor"), 1), :]
    keep = jnp.where(ids != PAD, doc_len**-0.5, 0.0)
    sides = mine_ref[...] + other_ref[...]
    in_side, out_side = (
        jnp.concatenate([sides[:, c * pair + at : c * pair + at + rank] for c in range(checkpoints)], axis=1)
        for at in (0, rank)
    )
    sums = jnp.dot(
        out_side.T * keep, in_side, precision=lax.Precision.HIGHEST, preferred_element_type=jnp.float32
    )
    grads = jnp.concatenate(
        [sums[c * rank : (c + 1) * rank, c * rank : (c + 1) * rank] for c in range(checkpoints)], axis=1
    )
    for j in range(dp):
        for k in range(tensor):
            sent_ref[j * tensor + k] = grads[j * rows : (j + 1) * rows].astype(sent_ref.dtype)


def score_kernel(dp, checkpoints, terms_ref, queries_ref, listed_ref, sent_ref):
    all_docs, rows, lanes = terms_ref.shape
    rank = lanes // checkpoints
    docs = all_docs // dp
    terms = terms_ref[...].astype(jnp.float32)
    parts = [terms[:, r, :].astype(jnp.bfloat16) for r in range(rows)]
    part = None
    for c in range(checkpoints):
        grads = jnp.concatenate([p[:, c * rank : (c + 1) * rank] for p in parts], axis=1)
        term = lax.dot_general(grads, queries_ref[c], LAST, preferred_element_type=jnp.float32)
        part = term if part is None else part + term
    part = part * (1.0 / rank)
    places = listed_ref.shape[0]
    every = lax.broadcasted_iota(jnp.int32, part.shape, 0)
    weight = jnp.zeros(part.shape, jnp.float32)
    for k in range(places):
        weight += jnp.where(listed_ref[k : k + 1, :] == every, 1.0 / places, 0.0)
    own = jnp.sum(weight * part, axis=0, keepdims=True)
    lines = part.shape[1] // 128
    for line in range(lines):
        at = slice(line * 128, (line + 1) * 128)
        for j in range(dp):
            for doc in range(docs):
                n = j * docs + doc
                sent_ref[j, pl.ds(doc * lines + line, 1), :] = part[n : n + 1, at]
            sent_ref[j, pl.ds(docs * lines + line, 1), :] = own[:, at]


def total_kernel(parts_ref, scores_ref, listed_ref):
    docs, columns = scores_ref.shape
    lines = columns // 128
    total = parts_ref[0]
    for i in range(1, parts_ref.shape[0]):
        total += parts_ref[i]
    for line in range(lines):
        at = slice(line * 128, (line + 1) * 128)
        for doc in range(docs):
            n = doc * lines + line
            scores_ref[doc : doc + 1, at] = total[n : n + 1]
        n = docs * lines + line
        listed_ref[:, at] = total[n : n + 1]


def pair_body(dp, tensor, activations, out_grads, proj_in, proj_out, token_ids, queries, query_docs):
    checkpoints, tokens, _ = activations.shape
    rank = proj_in.shape[1]
    docs, doc_len = token_ids.shape
    rows = rank // dp
    own_queries = queries.shape[1]
    lanes = checkpoints * rank
    wide = activations.size + out_grads.size
    width = activations.shape[2] + out_grads.shape[2]
    f32 = jnp.float32

    near = (activations, out_grads, proj_in.T, proj_out.T, token_ids, queries, query_docs.T)
    mine, theirs, near_queries, near_listing = pl.pallas_call(
        functools.partial(project_kernel, doc_len),
        in_specs=[HBM] * 7,
        out_specs=[VMEM] * 4,
        out_shape=[
            pltpu.VMEM((doc_len, 2 * lanes), f32),
            pltpu.VMEM((doc_len, 2 * lanes), f32),
            pltpu.VMEM(queries.shape, queries.dtype),
            pltpu.VMEM(query_docs.shape[::-1], query_docs.dtype),
        ],
        scratch_shapes=[
            pltpu.VMEM((tokens // BLOCK, checkpoints, BLOCK, width), activations.dtype),
            pltpu.VMEM((2 * rank, width), proj_in.dtype),
            pltpu.VMEM((docs, doc_len, 2 * lanes), f32),
            pltpu.SMEM(token_ids.shape, token_ids.dtype),
            pltpu.SemaphoreType.DMA((tokens // BLOCK,)),
            pltpu.SemaphoreType.DMA((5,)),
        ],
        compiler_params=pltpu.CompilerParams(vmem_limit_bytes=44 << 20),
        cost_estimate=pl.CostEstimate(flops=2 * wide * rank, bytes_accessed=2 * wide, transcendentals=0),
        name="project",
    )(*(pltpu.with_memory_space_constraint(x, pltpu.HBM) for x in near))
    other = lax.ppermute(theirs, "tensor", [(0, 1), (1, 0)])
    sent = pl.pallas_call(
        functools.partial(grad_kernel, dp, tensor, checkpoints),
        in_specs=[VMEM] * 3,
        out_specs=VMEM,
        out_shape=jax.ShapeDtypeStruct((dp * tensor, rows, lanes), jnp.bfloat16),
        compiler_params=pltpu.CompilerParams(vmem_limit_bytes=4 << 20),
        name="doc_grads",
    )(token_ids, mine, other)
    terms = lax.all_to_all(sent, ("dp", "tensor"), 0, 0, tiled=True)
    parts = pl.pallas_call(
        functools.partial(score_kernel, dp, checkpoints),
        in_specs=[VMEM] * 3,
        out_specs=VMEM,
        out_shape=jax.ShapeDtypeStruct((dp, (docs + 1) * own_queries // 128, 128), f32),
        compiler_params=pltpu.CompilerParams(vmem_limit_bytes=8 << 20),
        name="partial_scores",
    )(terms, near_queries, near_listing)
    parts = lax.all_to_all(parts, "dp", 0, 0, tiled=True)
    scores, listed = pl.pallas_call(
        total_kernel,
        in_specs=[VMEM],
        out_specs=[VMEM] * 2,
        out_shape=[jax.ShapeDtypeStruct((docs, own_queries), f32), jax.ShapeDtypeStruct((1, own_queries), f32)],
        compiler_params=pltpu.CompilerParams(vmem_limit_bytes=4 << 20),
        name="totals",
    )(parts)
    return scores, listed.reshape(own_queries)


def sum_over_tensor(part, size):
    if size == 2:
        return part + lax.ppermute(part, "tensor", [(0, 1), (1, 0)])
    return lax.psum(part, "tensor")


def any_body(dp, tensor, activations, out_grads, proj_in, proj_out, token_ids, queries, query_docs):
    checkpoints = activations.shape[0]
    rank = proj_in.shape[1]
    docs, doc_len = token_ids.shape
    rows = rank // dp
    own_queries = queries.shape[1]

    out_part = jnp.einsum("ctd,dr->ctr", out_grads, proj_out, preferred_element_type=jnp.float32)
    out_proj = sum_over_tensor(out_part, tensor)
    in_part = jnp.einsum("ctf,fr->ctr", activations, proj_in, preferred_element_type=jnp.float32)
    keep = (token_ids != PAD).astype(jnp.float32).reshape(1, docs, doc_len, 1)
    out_proj = out_proj.reshape(checkpoints, docs, doc_len, rank) * keep
    in_part = in_part.reshape(checkpoints, docs, doc_len, rank)
    term = jnp.einsum("cntr,cnts->crns", out_proj, in_part, precision=lax.Precision.HIGHEST)
    term = term.reshape(checkpoints, dp, 1, rows, docs * rank).transpose(1, 2, 0, 3, 4)
    term = jnp.broadcast_to(term, (dp, tensor, checkpoints, rows, docs * rank))
    term = term.reshape(dp * tensor, checkpoints, rows, docs * rank)
    terms = lax.all_to_all(term, ("dp", "tensor"), 0, 0, tiled=True)
    grads = terms.reshape(dp, tensor, checkpoints, rows, docs, rank).sum(1) * doc_len ** (-0.5)
    grads = grads.astype(jnp.bfloat16).transpose(1, 0, 3, 2, 4).reshape(checkpoints, dp * docs, rows * rank)

    part = jnp.einsum("cnf,cqf->nq", grads, queries, preferred_element_type=jnp.float32)
    every_doc = jnp.arange(dp * docs, dtype=jnp.int32)
    listing = (query_docs.T[None] == every_doc[:, None, None]).sum(1).astype(jnp.float32)
    listed_part = (listing * part).sum(0)
    sent = jnp.concatenate(
        [
            part.reshape(dp, docs, own_queries),
            jnp.broadcast_to(listed_part, (dp, 1, own_queries)),
        ],
        axis=1,
    )
    total = lax.all_to_all(sent, "dp", 0, 0, tiled=True).sum(0) / rank
    return total[:docs], total[docs] / query_docs.shape[1]


def solution(mesh):
    dp, tensor = mesh.shape["dp"], mesh.shape["tensor"]

    def body(*arrays):
        docs, doc_len = arrays[4].shape
        whole_tiles = all(n % 128 == 0 for n in (arrays[0].shape[2], arrays[1].shape[2], arrays[5].shape[1]))
        paired = tensor == 2 and docs == 2 and doc_len % (STEP * BLOCK) == 0 and whole_tiles
        return (pair_body if paired else any_body)(dp, tensor, *arrays)

    in_specs = (
        P(None, ("parts", "dp"), "tensor"),
        P(None, ("parts", "dp"), "tensor"),
        P("tensor", None),
        P("tensor", None),
        P(("parts", "dp"), None),
        P(None, "tensor", "dp"),
        P(("parts", "tensor"), None),
    )
    out_specs = (P(("parts", "dp"), "tensor"), P(("parts", "tensor")))
    return jax.shard_map(
        body,
        mesh=mesh,
        in_specs=in_specs,
        out_specs=out_specs,
        check_vma=False,
    )
```

```python
import functools

import jax
import jax.numpy as jnp
from jax import lax
from jax.experimental import pallas as pl
from jax.experimental.pallas import tpu as pltpu
from jax.sharding import PartitionSpec as P

PAD = 151643
BLOCK = 32
STEP = 2
VMEM = pl.BlockSpec(memory_space=pltpu.VMEM)
HBM = pl.BlockSpec(memory_space=pltpu.HBM)
LAST = (((1,), (1,)), ((), ()))


def project_kernel(
    doc_len, acts_ref, outs_ref, in_ref, out_ref, ids_ref, queries_ref, listing_ref,
    mine_ref, theirs_ref, near_queries_ref, near_listing_ref, wide, factor, found_both, ids, wide_sems, sems
):
    checkpoints, tokens, in_width = acts_ref.shape
    rank, out_width = out_ref.shape
    docs = tokens // doc_len
    blocks = doc_len // BLOCK
    keeps = lax.axis_index("tensor")
    in_cut, out_cut = pl.ds(0, in_width), pl.ds(in_width, out_width)

    def place(i, first):
        doc = jnp.where(i < first, 0, 1)
        return doc, i - doc * first

    def block_copies(i, doc, block):
        slot = i + 1
        rows = pl.ds(pl.multiple_of(doc * doc_len + block * BLOCK, BLOCK), BLOCK)
        return [
            pltpu.make_async_copy(source.at[:, rows], wide.at[slot, :, :, cut], wide_sems.at[slot])
            for source, cut in ((acts_ref, in_cut), (outs_ref, out_cut))
        ]

    def start(copies):
        for copy in copies:
            copy.start()

    def wait(copies):
        for copy in copies:
            copy.wait()

    ids_copy = pltpu.make_async_copy(ids_ref, ids, sems.at[0])
    factor_copies = [
        pltpu.make_async_copy(in_ref, factor.at[pl.ds(0, rank), in_cut], sems.at[1]),
        pltpu.make_async_copy(out_ref, factor.at[pl.ds(rank, rank), out_cut], sems.at[2]),
    ]
    late_copies = [
        pltpu.make_async_copy(queries_ref, near_queries_ref, sems.at[3]),
        pltpu.make_async_copy(listing_ref, near_listing_ref, sems.at[4]),
    ]

    ids_copy.start()
    start(factor_copies)
    for block in range(STEP):
        start(block_copies(block, 0, block))
    factor[:rank, in_width:] = jnp.zeros((rank, out_width), factor.dtype)
    factor[rank:, :in_width] = jnp.zeros((rank, in_width), factor.dtype)
    ids_copy.wait()
    first, second = (
        sum((ids[doc, block * BLOCK] != PAD).astype(jnp.int32) for block in range(blocks)) for doc in range(docs)
    )

    total = first + second

    def start_block(i, carry):
        start(block_copies(i, *place(i, first)))
        return carry

    lax.fori_loop(STEP, total, start_block, 0)
    start(late_copies)

    found_both[...] = jnp.zeros_like(found_both)

    def put(i, found):
        doc, block = place(i, first)
        line = jnp.concatenate([found[c * BLOCK : (c + 1) * BLOCK] for c in range(checkpoints)], axis=1)
        at = pl.ds(pl.multiple_of(block * BLOCK, BLOCK), BLOCK)

        found_both[jnp.where(doc == keeps, 0, 1), at] = line

    def wait_block(i):
        slot = wide.at[i + 1]
        pltpu.make_async_copy(slot, slot, wide_sems.at[i + 1]).wait()

    odd = lax.rem(total, STEP)

    def step(j, carry):
        i = j * STEP - odd
        pl.when(i >= 0)(lambda: wait_block(i))
        wait_block(i + 1)
        rows = checkpoints * BLOCK
        found = lax.dot_general(
            wide[pl.ds(i + 1, STEP)].reshape(STEP * rows, in_width + out_width),
            factor[...],
            LAST,
            preferred_element_type=jnp.float32,
        )
        pl.when(i >= 0)(lambda: put(i, found[:rows]))
        put(i + 1, found[rows:])
        return carry

    wait(factor_copies)
    lax.fori_loop(0, (total + odd) // STEP, step, 0)
    mine_ref[...] = found_both[0]
    theirs_ref[...] = found_both[1]
    wait(late_copies)


def grad_kernel(dp, tensor, checkpoints, ids_ref, mine_ref, other_ref, sent_ref):
    doc_len, lanes = mine_ref.shape
    pair = lanes // checkpoints
    rank = pair // 2
    rows = rank // dp
    ids = ids_ref[pl.ds(lax.axis_index("tensor"), 1), :]
    keep = jnp.where(ids != PAD, doc_len**-0.5, 0.0)
    sides = mine_ref[...] + other_ref[...]
    in_side, out_side = (
        jnp.concatenate([sides[:, c * pair + at : c * pair + at + rank] for c in range(checkpoints)], axis=1)
        for at in (0, rank)
    )
    sums = jnp.dot(
        out_side.T * keep, in_side, precision=lax.Precision.HIGHEST, preferred_element_type=jnp.float32
    )
    grads = jnp.concatenate(
        [sums[c * rank : (c + 1) * rank, c * rank : (c + 1) * rank] for c in range(checkpoints)], axis=1
    )
    for j in range(dp):
        for k in range(tensor):
            sent_ref[j * tensor + k] = grads[j * rows : (j + 1) * rows].astype(sent_ref.dtype)


def score_kernel(dp, checkpoints, terms_ref, queries_ref, listed_ref, sent_ref):
    all_docs, rows, lanes = terms_ref.shape
    rank = lanes // checkpoints
    docs = all_docs // dp
    terms = terms_ref[...].astype(jnp.float32)
    parts = [terms[:, r, :].astype(jnp.bfloat16) for r in range(rows)]
    part = None
    for c in range(checkpoints):
        grads = jnp.concatenate([p[:, c * rank : (c + 1) * rank] for p in parts], axis=1)
        term = lax.dot_general(grads, queries_ref[c], LAST, preferred_element_type=jnp.float32)
        part = term if part is None else part + term
    part = part * (1.0 / rank)
    places = listed_ref.shape[0]
    every = lax.broadcasted_iota(jnp.int32, part.shape, 0)
    weight = jnp.zeros(part.shape, jnp.float32)
    for k in range(places):
        weight += jnp.where(listed_ref[k : k + 1, :] == every, 1.0 / places, 0.0)
    own = jnp.sum(weight * part, axis=0, keepdims=True)
    lines = part.shape[1] // 128
    for line in range(lines):
        at = slice(line * 128, (line + 1) * 128)
        for j in range(dp):
            for doc in range(docs):
                n = j * docs + doc
                sent_ref[j, pl.ds(doc * lines + line, 1), :] = part[n : n + 1, at]
            sent_ref[j, pl.ds(docs * lines + line, 1), :] = own[:, at]


def total_kernel(parts_ref, scores_ref, listed_ref):
    docs, columns = scores_ref.shape
    lines = columns // 128
    total = parts_ref[0]
    for i in range(1, parts_ref.shape[0]):
        total += parts_ref[i]
    for line in range(lines):
        at = slice(line * 128, (line + 1) * 128)
        for doc in range(docs):
            n = doc * lines + line
            scores_ref[doc : doc + 1, at] = total[n : n + 1]
        n = docs * lines + line
        listed_ref[:, at] = total[n : n + 1]


def pair_body(dp, tensor, activations, out_grads, proj_in, proj_out, token_ids, queries, query_docs):
    checkpoints, tokens, _ = activations.shape
    rank = proj_in.shape[1]
    docs, doc_len = token_ids.shape
    rows = rank // dp
    own_queries = queries.shape[1]
    lanes = checkpoints * rank
    wide = activations.size + out_grads.size
    width = activations.shape[2] + out_grads.shape[2]
    f32 = jnp.float32

    near = (activations, out_grads, proj_in.T, proj_out.T, token_ids, queries, query_docs.T)
    mine, theirs, near_queries, near_listing = pl.pallas_call(
        functools.partial(project_kernel, doc_len),
        in_specs=[HBM] * 7,
        out_specs=[VMEM] * 4,
        out_shape=[
            pltpu.VMEM((doc_len, 2 * lanes), f32),
            pltpu.VMEM((doc_len, 2 * lanes), f32),
            pltpu.VMEM(queries.shape, queries.dtype),
            pltpu.VMEM(query_docs.shape[::-1], query_docs.dtype),
        ],
        scratch_shapes=[
            pltpu.VMEM((tokens // BLOCK + 1, checkpoints, BLOCK, width), activations.dtype),
            pltpu.VMEM((2 * rank, width), proj_in.dtype),
            pltpu.VMEM((docs, doc_len, 2 * lanes), f32),
            pltpu.SMEM(token_ids.shape, token_ids.dtype),
            pltpu.SemaphoreType.DMA((tokens // BLOCK + 1,)),
            pltpu.SemaphoreType.DMA((5,)),
        ],
        compiler_params=pltpu.CompilerParams(vmem_limit_bytes=46 << 20),
        cost_estimate=pl.CostEstimate(flops=2 * wide * rank, bytes_accessed=2 * wide, transcendentals=0),
        name="project",
    )(*(pltpu.with_memory_space_constraint(x, pltpu.HBM) for x in near))
    other = lax.ppermute(theirs, "tensor", [(0, 1), (1, 0)])
    sent = pl.pallas_call(
        functools.partial(grad_kernel, dp, tensor, checkpoints),
        in_specs=[VMEM] * 3,
        out_specs=VMEM,
        out_shape=jax.ShapeDtypeStruct((dp * tensor, rows, lanes), jnp.bfloat16),
        compiler_params=pltpu.CompilerParams(vmem_limit_bytes=4 << 20),
        name="doc_grads",
    )(token_ids, mine, other)
    terms = lax.all_to_all(sent, ("dp", "tensor"), 0, 0, tiled=True)
    parts = pl.pallas_call(
        functools.partial(score_kernel, dp, checkpoints),
        in_specs=[VMEM] * 3,
        out_specs=VMEM,
        out_shape=jax.ShapeDtypeStruct((dp, (docs + 1) * own_queries // 128, 128), f32),
        compiler_params=pltpu.CompilerParams(vmem_limit_bytes=8 << 20),
        name="partial_scores",
    )(terms, near_queries, near_listing)
    parts = lax.all_to_all(parts, "dp", 0, 0, tiled=True)
    scores, listed = pl.pallas_call(
        total_kernel,
        in_specs=[VMEM],
        out_specs=[VMEM] * 2,
        out_shape=[jax.ShapeDtypeStruct((docs, own_queries), f32), jax.ShapeDtypeStruct((1, own_queries), f32)],
        compiler_params=pltpu.CompilerParams(vmem_limit_bytes=4 << 20),
        name="totals",
    )(parts)
    return scores, listed.reshape(own_queries)


def sum_over_tensor(part, size):
    if size == 2:
        return part + lax.ppermute(part, "tensor", [(0, 1), (1, 0)])
    return lax.psum(part, "tensor")


def any_body(dp, tensor, activations, out_grads, proj_in, proj_out, token_ids, queries, query_docs):
    checkpoints = activations.shape[0]
    rank = proj_in.shape[1]
    docs, doc_len = token_ids.shape
    rows = rank // dp
    own_queries = queries.shape[1]

    out_part = jnp.einsum("ctd,dr->ctr", out_grads, proj_out, preferred_element_type=jnp.float32)
    out_proj = sum_over_tensor(out_part, tensor)
    in_part = jnp.einsum("ctf,fr->ctr", activations, proj_in, preferred_element_type=jnp.float32)
    keep = (token_ids != PAD).astype(jnp.float32).reshape(1, docs, doc_len, 1)
    out_proj = out_proj.reshape(checkpoints, docs, doc_len, rank) * keep
    in_part = in_part.reshape(checkpoints, docs, doc_len, rank)
    term = jnp.einsum("cntr,cnts->crns", out_proj, in_part, precision=lax.Precision.HIGHEST)
    term = term.reshape(checkpoints, dp, 1, rows, docs * rank).transpose(1, 2, 0, 3, 4)
    term = jnp.broadcast_to(term, (dp, tensor, checkpoints, rows, docs * rank))
    term = term.reshape(dp * tensor, checkpoints, rows, docs * rank)
    terms = lax.all_to_all(term, ("dp", "tensor"), 0, 0, tiled=True)
    grads = terms.reshape(dp, tensor, checkpoints, rows, docs, rank).sum(1) * doc_len ** (-0.5)
    grads = grads.astype(jnp.bfloat16).transpose(1, 0, 3, 2, 4).reshape(checkpoints, dp * docs, rows * rank)

    part = jnp.einsum("cnf,cqf->nq", grads, queries, preferred_element_type=jnp.float32)
    every_doc = jnp.arange(dp * docs, dtype=jnp.int32)
    listing = (query_docs.T[None] == every_doc[:, None, None]).sum(1).astype(jnp.float32)
    listed_part = (listing * part).sum(0)
    sent = jnp.concatenate(
        [
            part.reshape(dp, docs, own_queries),
            jnp.broadcast_to(listed_part, (dp, 1, own_queries)),
        ],
        axis=1,
    )
    total = lax.all_to_all(sent, "dp", 0, 0, tiled=True).sum(0) / rank
    return total[:docs], total[docs] / query_docs.shape[1]


def solution(mesh):
    dp, tensor = mesh.shape["dp"], mesh.shape["tensor"]

    def body(*arrays):
        docs, doc_len = arrays[4].shape
        whole_tiles = all(n % 128 == 0 for n in (arrays[0].shape[2], arrays[1].shape[2], arrays[5].shape[1]))
        paired = tensor == 2 and docs == 2 and doc_len % (STEP * BLOCK) == 0 and whole_tiles
        return (pair_body if paired else any_body)(dp, tensor, *arrays)

    in_specs = (
        P(None, ("parts", "dp"), "tensor"),
        P(None, ("parts", "dp"), "tensor"),
        P("tensor", None),
        P("tensor", None),
        P(("parts", "dp"), None),
        P(None, "tensor", "dp"),
        P(("parts", "tensor"), None),
    )
    out_specs = (P(("parts", "dp"), "tensor"), P(("parts", "tensor")))
    return jax.shard_map(
        body,
        mesh=mesh,
        in_specs=in_specs,
        out_specs=out_specs,
        check_vma=False,
    )
```

```python
import functools

import jax
import jax.numpy as jnp
from jax import lax
from jax.experimental import pallas as pl
from jax.experimental.pallas import tpu as pltpu
from jax.sharding import PartitionSpec as P

PAD = 151643
BLOCK = 32
STEP = 2
VMEM = pl.BlockSpec(memory_space=pltpu.VMEM)
HBM = pl.BlockSpec(memory_space=pltpu.HBM)
LAST = (((1,), (1,)), ((), ()))


def project_kernel(
    doc_len, acts_ref, outs_ref, in_ref, out_ref, ids_ref, queries_ref, listing_ref,
    mine_ref, theirs_ref, near_queries_ref, near_listing_ref, wide, factor, found_both, ids, wide_sems, sems
):
    checkpoints, tokens, in_width = acts_ref.shape
    rank, out_width = out_ref.shape
    docs = tokens // doc_len
    blocks = doc_len // BLOCK
    keeps = lax.axis_index("tensor")
    in_cut, out_cut = pl.ds(0, in_width), pl.ds(in_width, out_width)

    def place(i, first):
        doc = jnp.where(i < first, 0, 1)
        return doc, i - doc * first

    def block_copies(i, doc, block, sem):
        slot = i + 1
        rows = pl.ds(pl.multiple_of(doc * doc_len + block * BLOCK, BLOCK), BLOCK)
        return [
            pltpu.make_async_copy(source.at[:, rows], wide.at[slot, :, :, cut], wide_sems.at[sem])
            for source, cut in ((acts_ref, in_cut), (outs_ref, out_cut))
        ]

    def start(copies):
        for copy in copies:
            copy.start()

    def wait(copies):
        for copy in copies:
            copy.wait()

    ids_copy = pltpu.make_async_copy(ids_ref, ids, sems.at[0])
    factor_copies = [
        pltpu.make_async_copy(in_ref, factor.at[pl.ds(0, rank), in_cut], sems.at[1]),
        pltpu.make_async_copy(out_ref, factor.at[pl.ds(rank, rank), out_cut], sems.at[2]),
    ]
    late_copies = [
        pltpu.make_async_copy(queries_ref, near_queries_ref, sems.at[3]),
        pltpu.make_async_copy(listing_ref, near_listing_ref, sems.at[4]),
    ]

    ids_copy.start()
    start(factor_copies)
    for block in range(STEP):
        start(block_copies(block, 0, block, block))
    factor[:rank, in_width:] = jnp.zeros((rank, out_width), factor.dtype)
    factor[rank:, :in_width] = jnp.zeros((rank, in_width), factor.dtype)
    ids_copy.wait()
    first, second = (
        sum((ids[doc, block * BLOCK] != PAD).astype(jnp.int32) for block in range(blocks)) for doc in range(docs)
    )

    total = first + second
    odd = lax.rem(total, STEP)

    def start_block(i, carry):
        start(block_copies(i, *place(i, first), STEP + (i + odd) // STEP))
        return carry

    lax.fori_loop(STEP, total, start_block, 0)
    start(late_copies)

    found_both[...] = jnp.zeros_like(found_both)

    def put(i, found):
        doc, block = place(i, first)
        line = jnp.concatenate([found[c * BLOCK : (c + 1) * BLOCK] for c in range(checkpoints)], axis=1)
        at = pl.ds(pl.multiple_of(block * BLOCK, BLOCK), BLOCK)

        found_both[jnp.where(doc == keeps, 0, 1), at] = line

    def wait_slots(i, count, sem):
        slots = wide.at[pl.ds(i + 1, count)]
        pltpu.make_async_copy(slots, slots, wide_sems.at[sem]).wait()

    def step(j, carry):
        i = j * STEP - odd

        @pl.when(i < STEP)
        def _():
            pl.when(i >= 0)(lambda: wait_slots(i, 1, i))
            wait_slots(i + 1, 1, jnp.where(i + 1 < STEP, i + 1, STEP + j))

        pl.when(i >= STEP)(lambda: wait_slots(i, STEP, STEP + j))
        rows = checkpoints * BLOCK
        found = lax.dot_general(
            wide[pl.ds(i + 1, STEP)].reshape(STEP * rows, in_width + out_width),
            factor[...],
            LAST,
            preferred_element_type=jnp.float32,
        )
        pl.when(i >= 0)(lambda: put(i, found[:rows]))
        put(i + 1, found[rows:])
        return carry

    wait(factor_copies)
    lax.fori_loop(0, (total + odd) // STEP, step, 0)
    mine_ref[...] = found_both[0]
    theirs_ref[...] = found_both[1]
    wait(late_copies)


def grad_kernel(dp, tensor, checkpoints, ids_ref, mine_ref, other_ref, sent_ref):
    doc_len, lanes = mine_ref.shape
    pair = lanes // checkpoints
    rank = pair // 2
    rows = rank // dp
    ids = ids_ref[pl.ds(lax.axis_index("tensor"), 1), :]
    keep = jnp.where(ids != PAD, doc_len**-0.5, 0.0)
    sides = mine_ref[...] + other_ref[...]
    in_side, out_side = (
        jnp.concatenate([sides[:, c * pair + at : c * pair + at + rank] for c in range(checkpoints)], axis=1)
        for at in (0, rank)
    )
    sums = jnp.dot(
        out_side.T * keep, in_side, precision=lax.Precision.HIGHEST, preferred_element_type=jnp.float32
    )
    grads = jnp.concatenate(
        [sums[c * rank : (c + 1) * rank, c * rank : (c + 1) * rank] for c in range(checkpoints)], axis=1
    )
    for j in range(dp):
        for k in range(tensor):
            sent_ref[j * tensor + k] = grads[j * rows : (j + 1) * rows].astype(sent_ref.dtype)


def score_kernel(dp, checkpoints, terms_ref, queries_ref, listed_ref, sent_ref):
    all_docs, rows, lanes = terms_ref.shape
    rank = lanes // checkpoints
    docs = all_docs // dp
    terms = terms_ref[...].astype(jnp.float32)
    parts = [terms[:, r, :].astype(jnp.bfloat16) for r in range(rows)]
    part = None
    for c in range(checkpoints):
        grads = jnp.concatenate([p[:, c * rank : (c + 1) * rank] for p in parts], axis=1)
        term = lax.dot_general(grads, queries_ref[c], LAST, preferred_element_type=jnp.float32)
        part = term if part is None else part + term
    part = part * (1.0 / rank)
    places = listed_ref.shape[0]
    every = lax.broadcasted_iota(jnp.int32, part.shape, 0)
    weight = jnp.zeros(part.shape, jnp.float32)
    for k in range(places):
        weight += jnp.where(listed_ref[k : k + 1, :] == every, 1.0 / places, 0.0)
    own = jnp.sum(weight * part, axis=0, keepdims=True)
    lines = part.shape[1] // 128
    for line in range(lines):
        at = slice(line * 128, (line + 1) * 128)
        for j in range(dp):
            for doc in range(docs):
                n = j * docs + doc
                sent_ref[j, pl.ds(doc * lines + line, 1), :] = part[n : n + 1, at]
            sent_ref[j, pl.ds(docs * lines + line, 1), :] = own[:, at]


def total_kernel(parts_ref, scores_ref, listed_ref):
    docs, columns = scores_ref.shape
    lines = columns // 128
    total = parts_ref[0]
    for i in range(1, parts_ref.shape[0]):
        total += parts_ref[i]
    for line in range(lines):
        at = slice(line * 128, (line + 1) * 128)
        for doc in range(docs):
            n = doc * lines + line
            scores_ref[doc : doc + 1, at] = total[n : n + 1]
        n = docs * lines + line
        listed_ref[:, at] = total[n : n + 1]


def pair_body(dp, tensor, activations, out_grads, proj_in, proj_out, token_ids, queries, query_docs):
    checkpoints, tokens, _ = activations.shape
    rank = proj_in.shape[1]
    docs, doc_len = token_ids.shape
    rows = rank // dp
    own_queries = queries.shape[1]
    lanes = checkpoints * rank
    wide = activations.size + out_grads.size
    width = activations.shape[2] + out_grads.shape[2]
    f32 = jnp.float32

    near = (activations, out_grads, proj_in.T, proj_out.T, token_ids, queries, query_docs.T)
    mine, theirs, near_queries, near_listing = pl.pallas_call(
        functools.partial(project_kernel, doc_len),
        in_specs=[HBM] * 7,
        out_specs=[VMEM] * 4,
        out_shape=[
            pltpu.VMEM((doc_len, 2 * lanes), f32),
            pltpu.VMEM((doc_len, 2 * lanes), f32),
            pltpu.VMEM(queries.shape, queries.dtype),
            pltpu.VMEM(query_docs.shape[::-1], query_docs.dtype),
        ],
        scratch_shapes=[
            pltpu.VMEM((tokens // BLOCK + 1, checkpoints, BLOCK, width), activations.dtype),
            pltpu.VMEM((2 * rank, width), proj_in.dtype),
            pltpu.VMEM((docs, doc_len, 2 * lanes), f32),
            pltpu.SMEM(token_ids.shape, token_ids.dtype),
            pltpu.SemaphoreType.DMA((STEP + tokens // (STEP * BLOCK),)),
            pltpu.SemaphoreType.DMA((5,)),
        ],
        compiler_params=pltpu.CompilerParams(vmem_limit_bytes=46 << 20),
        cost_estimate=pl.CostEstimate(flops=2 * wide * rank, bytes_accessed=2 * wide, transcendentals=0),
        name="project",
    )(*(pltpu.with_memory_space_constraint(x, pltpu.HBM) for x in near))
    other = lax.ppermute(theirs, "tensor", [(0, 1), (1, 0)])
    sent = pl.pallas_call(
        functools.partial(grad_kernel, dp, tensor, checkpoints),
        in_specs=[VMEM] * 3,
        out_specs=VMEM,
        out_shape=jax.ShapeDtypeStruct((dp * tensor, rows, lanes), jnp.bfloat16),
        compiler_params=pltpu.CompilerParams(vmem_limit_bytes=4 << 20),
        name="doc_grads",
    )(token_ids, mine, other)
    terms = lax.all_to_all(sent, ("dp", "tensor"), 0, 0, tiled=True)
    parts = pl.pallas_call(
        functools.partial(score_kernel, dp, checkpoints),
        in_specs=[VMEM] * 3,
        out_specs=VMEM,
        out_shape=jax.ShapeDtypeStruct((dp, (docs + 1) * own_queries // 128, 128), f32),
        compiler_params=pltpu.CompilerParams(vmem_limit_bytes=8 << 20),
        name="partial_scores",
    )(terms, near_queries, near_listing)
    parts = lax.all_to_all(parts, "dp", 0, 0, tiled=True)
    scores, listed = pl.pallas_call(
        total_kernel,
        in_specs=[VMEM],
        out_specs=[VMEM] * 2,
        out_shape=[jax.ShapeDtypeStruct((docs, own_queries), f32), jax.ShapeDtypeStruct((1, own_queries), f32)],
        compiler_params=pltpu.CompilerParams(vmem_limit_bytes=4 << 20),
        name="totals",
    )(parts)
    return scores, listed.reshape(own_queries)


def sum_over_tensor(part, size):
    if size == 2:
        return part + lax.ppermute(part, "tensor", [(0, 1), (1, 0)])
    return lax.psum(part, "tensor")


def any_body(dp, tensor, activations, out_grads, proj_in, proj_out, token_ids, queries, query_docs):
    checkpoints = activations.shape[0]
    rank = proj_in.shape[1]
    docs, doc_len = token_ids.shape
    rows = rank // dp
    own_queries = queries.shape[1]

    out_part = jnp.einsum("ctd,dr->ctr", out_grads, proj_out, preferred_element_type=jnp.float32)
    out_proj = sum_over_tensor(out_part, tensor)
    in_part = jnp.einsum("ctf,fr->ctr", activations, proj_in, preferred_element_type=jnp.float32)
    keep = (token_ids != PAD).astype(jnp.float32).reshape(1, docs, doc_len, 1)
    out_proj = out_proj.reshape(checkpoints, docs, doc_len, rank) * keep
    in_part = in_part.reshape(checkpoints, docs, doc_len, rank)
    term = jnp.einsum("cntr,cnts->crns", out_proj, in_part, precision=lax.Precision.HIGHEST)
    term = term.reshape(checkpoints, dp, 1, rows, docs * rank).transpose(1, 2, 0, 3, 4)
    term = jnp.broadcast_to(term, (dp, tensor, checkpoints, rows, docs * rank))
    term = term.reshape(dp * tensor, checkpoints, rows, docs * rank)
    terms = lax.all_to_all(term, ("dp", "tensor"), 0, 0, tiled=True)
    grads = terms.reshape(dp, tensor, checkpoints, rows, docs, rank).sum(1) * doc_len ** (-0.5)
    grads = grads.astype(jnp.bfloat16).transpose(1, 0, 3, 2, 4).reshape(checkpoints, dp * docs, rows * rank)

    part = jnp.einsum("cnf,cqf->nq", grads, queries, preferred_element_type=jnp.float32)
    every_doc = jnp.arange(dp * docs, dtype=jnp.int32)
    listing = (query_docs.T[None] == every_doc[:, None, None]).sum(1).astype(jnp.float32)
    listed_part = (listing * part).sum(0)
    sent = jnp.concatenate(
        [
            part.reshape(dp, docs, own_queries),
            jnp.broadcast_to(listed_part, (dp, 1, own_queries)),
        ],
        axis=1,
    )
    total = lax.all_to_all(sent, "dp", 0, 0, tiled=True).sum(0) / rank
    return total[:docs], total[docs] / query_docs.shape[1]


def solution(mesh):
    dp, tensor = mesh.shape["dp"], mesh.shape["tensor"]

    def body(*arrays):
        docs, doc_len = arrays[4].shape
        whole_tiles = all(n % 128 == 0 for n in (arrays[0].shape[2], arrays[1].shape[2], arrays[5].shape[1]))
        paired = tensor == 2 and docs == 2 and doc_len % (STEP * BLOCK) == 0 and whole_tiles
        return (pair_body if paired else any_body)(dp, tensor, *arrays)

    in_specs = (
        P(None, ("parts", "dp"), "tensor"),
        P(None, ("parts", "dp"), "tensor"),
        P("tensor", None),
        P("tensor", None),
        P(("parts", "dp"), None),
        P(None, "tensor", "dp"),
        P(("parts", "tensor"), None),
    )
    out_specs = (P(("parts", "dp"), "tensor"), P(("parts", "tensor")))
    return jax.shard_map(
        body,
        mesh=mesh,
        in_specs=in_specs,
        out_specs=out_specs,
        check_vma=False,
    )
```
